32 devices in a mesh: section: 4 (over y, x), seq: 8 (over z, core).
Axes of the slice: x: 2, y: 2, z: 4, core: 2. Of those that a mesh axis runs over, the one named last changes fastest.
Arguments:
- queries: bfloat16 [4, 2048, 2048], P('section', 'seq'), may hold values from -24 to 24
- keys: bfloat16 [4, 2048, 1024], P('section', 'seq'), may hold values from -24 to 24
- values: bfloat16 [4, 2048, 1024], P('section', 'seq'), may hold values from -6 to 6
- segment_ids: int32 [2048], P('seq'), may hold values from 0 to 3, as said below
- positions: int32 [2048], P('seq'), may hold values from 0 to 1023, as said below
- residual_in: bfloat16 [2048, 2048], P('seq'), may hold values from -6 to 6
- post_gain: float32 [4, 2048], P('section'), may hold values from 0.1 to 1.9
Outputs:
- layer_out: bfloat16 [4, 2048, 2048], P('section', 'seq')
The draws below stay inside these ranges and needn't reach their ends.
Inputs may be any that keep to these rules, and one draw needn't show every extreme that they name: `segment_ids`: never falling; each document holds 1 to 1024 tokens, one exactly 1024. `positions`: the token's index minus the index of the first token of its document.
All inputs are finite; a program needn't handle non-finite values.
Results may differ from the reference program's by a relative error of at most 0.011.
Values may be sent and summed in bfloat16 or wider, within the bound.
A program may use at most 128 MiB of HBM per device.

```python
import math
import jax
import jax.numpy as jnp
from jax import lax

HQ = 8
HK = 4
HD = 256
WINDOW = 4096
TOK_DEV = 256
LAYERS = 4
TOKENS = 2048
DOC_LIMIT = 1024
DOCS = 4


def lifted_heads(key, heads):
    base_key, lift_key = jax.random.split(key)
    base = jax.random.truncated_normal(base_key, -6.0, 6.0, (LAYERS, TOKENS, heads, HD), jnp.float32)
    lift = jnp.exp(jax.random.uniform(lift_key, (LAYERS, TOKENS, heads, 1), jnp.float32, 0.0, math.log(4.0)))
    return (base * lift).reshape(LAYERS, TOKENS, heads * HD).astype(jnp.bfloat16)


def draw_queries(key, part):
    return lifted_heads(jax.random.fold_in(key, 101), HQ)


def draw_keys(key, part):
    return lifted_heads(jax.random.fold_in(key, 202), HK)


def document_layout(key):
    shared = jax.random.fold_in(key, 303)
    place_key, shift_key = jax.random.split(shared)
    others = DOCS - 1
    rest = TOKENS - DOC_LIMIT
    base = rest // others
    reach = max(base // 4, 0)
    shifts = jax.random.randint(shift_key, (others,), -reach, reach + 1).astype(jnp.int32)
    lengths_other = base + shifts - jnp.roll(shifts, 1)
    lengths_other = lengths_other.at[others - 1].add(rest - base * others)
    place = jax.random.randint(place_key, (), 0, DOCS).astype(jnp.int32)
    slot = jnp.arange(DOCS, dtype=jnp.int32)
    before = lengths_other[jnp.clip(slot, 0, others - 1)]
    after = lengths_other[jnp.clip(slot - 1, 0, others - 1)]
    lengths = jnp.where(slot < place, before, jnp.where(slot == place, DOC_LIMIT, after)).astype(jnp.int32)
    ends = jnp.cumsum(lengths).astype(jnp.int32)
    starts = ends - lengths
    token = jnp.arange(TOKENS, dtype=jnp.int32)
    seg = jnp.sum((token[:, None] >= ends[None, :]).astype(jnp.int32), axis=1).astype(jnp.int32)
    hit = (seg[:, None] == slot[None, :]).astype(jnp.int32)
    first = jnp.sum(hit * starts[None, :], axis=1).astype(jnp.int32)
    return (seg, token - first)


def draw_segment_ids(key, part):
    return document_layout(key)[0]


def draw_positions(key, part):
    return document_layout(key)[1]


def level_of(key, dims, cuts, low, top_value):
    level = 1.0
    for dim, shards_of in cuts:
        heights = jax.random.uniform(jax.random.fold_in(jax.random.fold_in(key, 6), dim), (shards_of,), jnp.float32, low / len(cuts), top_value / len(cuts))
        level = level * jnp.repeat(jnp.exp(heights), dims[dim] // shards_of).reshape((-1,) + (1,) * (len(dims) - 1 - dim))
    return level


def centred(rng, extent, width, bound, cuts=(), kind=jnp.bfloat16):
    drawn = width * jax.random.normal(rng, extent, jnp.float32)
    if cuts:
        drawn = drawn * level_of(rng, extent, cuts, -0.22, 0.18)
    return jnp.clip(drawn, -bound, bound).astype(kind)


def setup_inputs(seed: int = 0) -> dict:
    key_of = jax.random.split(jax.random.key(seed), 8)
    queries = draw_queries(jax.random.fold_in(key_of[7], 71), 0)
    keys = draw_keys(jax.random.fold_in(key_of[7], 71), 0)
    values = centred(key_of[2], (LAYERS, TOKENS, HK * HD), 1.0, 6.0, ((0, 4), (1, 8)))
    segment_ids = draw_segment_ids(jax.random.fold_in(key_of[7], 71), 0)
    positions = draw_positions(jax.random.fold_in(key_of[7], 71), 0)
    residual_in = centred(key_of[5], (TOKENS, HQ * HD), 1.0, 6.0, ((0, 8),))
    post_gain = jnp.clip(1.0 + 0.18 * jax.random.normal(key_of[6], (LAYERS, HQ * HD), jnp.float32), 0.1, 1.9)
    return dict(queries=queries, keys=keys, values=values, segment_ids=segment_ids, positions=positions, residual_in=residual_in, post_gain=post_gain)


def rotate(x, position, heads):
    count = x.shape[0]
    half = HD // 2
    parts = x.astype(jnp.float32).reshape(count, heads, HD)
    inverse = jnp.exp(-math.log(10000.0) * jnp.arange(half).astype(jnp.float32) / half)
    angle = position.astype(jnp.float32)[:, None] * inverse[None, :]
    cosine = jnp.cos(angle)[:, None, :]
    sine = jnp.sin(angle)[:, None, :]
    first = parts[:, :, :half]
    second = parts[:, :, half:]
    turned = jnp.concatenate([first * cosine - second * sine, second * cosine + first * sine], axis=-1)
    return turned.reshape(count, heads * HD).astype(jnp.bfloat16)

def one_layer(query_rot, key_rot, value_layer, segment_ids, gain):
    group = HQ // HK
    key_pad = jnp.concatenate([jnp.zeros((WINDOW, HK * HD), jnp.bfloat16), key_rot], axis=0)
    value_pad = jnp.concatenate([jnp.zeros((WINDOW, HK * HD), jnp.bfloat16), value_layer], axis=0)
    seg_pad = jnp.concatenate([jnp.full((WINDOW,), -1, jnp.int32), segment_ids.astype(jnp.int32)], axis=0)
    span = WINDOW + TOK_DEV
    scale = HD ** (-0.5)

    def block(index):
        first = (index * TOK_DEV).astype(jnp.int32)
        query_blk = lax.dynamic_slice_in_dim(query_rot, first, TOK_DEV, 0).astype(jnp.float32)
        query_blk = query_blk.reshape(TOK_DEV, HK, group, HD)
        key_blk = lax.dynamic_slice_in_dim(key_pad, first, span, 0).astype(jnp.float32).reshape(span, HK, HD)
        value_blk = lax.dynamic_slice_in_dim(value_pad, first, span, 0).astype(jnp.float32).reshape(span, HK, HD)
        seg_key = lax.dynamic_slice_in_dim(seg_pad, first, span, 0)
        seg_query = lax.dynamic_slice_in_dim(segment_ids.astype(jnp.int32), first, TOK_DEV, 0)
        query_pos = first + jnp.arange(TOK_DEV).astype(jnp.int32)
        key_pos = first - WINDOW + jnp.arange(span).astype(jnp.int32)
        gap = query_pos[:, None] - key_pos[None, :]
        allowed = (key_pos[None, :] >= 0) & (gap >= 0) & (gap < WINDOW) & (seg_query[:, None] == seg_key[None, :])
        score = jnp.einsum('qgjd,kgd->qgjk', query_blk, key_blk) * scale
        score = 50.0 * jnp.tanh(score / 50.0)
        weight = jnp.where(allowed[:, None, None, :], jnp.exp(score), 0.0)
        total = lax.optimization_barrier(jnp.sum(weight, axis=-1))
        weight_b = weight.astype(jnp.bfloat16).astype(jnp.float32)
        summed = jnp.einsum('qgjk,kgd->qgjd', weight_b, value_blk)
        attended = (summed / total[..., None]).reshape(TOK_DEV, HQ * HD)
        norm = lax.rsqrt(lax.optimization_barrier(jnp.mean(attended * attended, axis=-1, keepdims=True)) + 1e-06)
        return attended * norm * gain[None, :]
    deltas = lax.map(block, jnp.arange(TOKENS // TOK_DEV).astype(jnp.int32))
    return deltas.reshape(TOKENS, HQ * HD)

def reference(queries, keys, values, segment_ids, positions, residual_in, post_gain):
    seg = segment_ids.astype(jnp.int32)
    position = positions.astype(jnp.int32)
    outputs = []
    running = residual_in.astype(jnp.float32)
    for layer in range(LAYERS):
        query_rot = rotate(queries[layer], position, HQ)
        key_rot = rotate(keys[layer], position, HK)
        delta = one_layer(query_rot, key_rot, values[layer], seg, post_gain[layer].astype(jnp.float32))
        running = running + delta
        outputs.append(running.astype(jnp.bfloat16))
    return jnp.stack(outputs, axis=0)
```

```python
import functools
import math

import jax
import jax.numpy as jnp
from jax import lax
from jax.experimental import pallas as pl
from jax.experimental.pallas import tpu as pltpu
from jax.sharding import PartitionSpec as P

HQ = 8
HK = 4
HD = 256
WINDOW = 4096
GROUP = HQ // HK
HALF = HD // 2
PAIR = GROUP * HD
MESH = pl.DeviceIdType.MESH
NT = (((1,), (1,)), ((), ()))
NN = (((1,), (0,)), ((), ()))


def kernel(
    seqs, secs, back, rows,
    q_ref, k_ref, v_ref, pos_ref, res_ref, gain_ref,
    out_ref,
    kv, qrot, cos_ref, sin_ref, low, acc, den, own, sent, got, gains,
    kv_send, kv_recv, att_send, att_recv, gain_send, gain_recv,
):
    me = lax.axis_index("seq")
    sec = lax.axis_index("section")

    barrier = pltpu.get_barrier_semaphore()

    @pl.when(me > 0)
    def _():
        pl.semaphore_signal(barrier, inc=1, device_id={"seq": me - 1}, device_id_type=MESH)

    for other in range(secs - 1):

        @pl.when(other < sec)
        def _(other=other):
            pl.semaphore_signal(barrier, inc=1, device_id={"section": other}, device_id_type=MESH)

    def kv_copy(step, head):
        return pltpu.make_async_remote_copy(
            src_ref=kv.at[step, head],
            dst_ref=kv.at[step + 1, head],
            send_sem=kv_send.at[step, head],
            recv_sem=kv_recv.at[step, head],
            device_id={"seq": me + 1},
            device_id_type=MESH,
        )

    def att_copy(source, head, target):
        return pltpu.make_async_remote_copy(
            src_ref=sent.at[head],
            dst_ref=got.at[source, head],
            send_sem=att_send.at[target - 1, head],
            recv_sem=att_recv.at[source, head],
            device_id={"section": target},
            device_id_type=MESH,
        )

    def gain_copy(source, target):
        return pltpu.make_async_remote_copy(
            src_ref=gains.at[secs - 1],
            dst_ref=gains.at[source],
            send_sem=gain_send.at[target - 1],
            recv_sem=gain_recv.at[source],
            device_id={"section": target},
            device_id_type=MESH,
        )

    def to_later(act):
        for target in range(1, secs):

            @pl.when(target > sec)
            def _(target=target):
                act(target)

    place = jnp.broadcast_to(pos_ref[...], (HALF, rows)).astype(jnp.float32).T
    lane = lax.broadcasted_iota(jnp.int32, (rows, HALF), 1).astype(jnp.float32)
    angle = place * jnp.exp(lane * (-math.log(10000.0) / HALF))
    cos_ref[...] = jnp.cos(angle)
    sin_ref[...] = jnp.sin(angle)
    gains[secs - 1] = jnp.broadcast_to(gain_ref[...], gains.shape[1:])

    def turned(ref, head):
        first = ref[0, :, head * HD : head * HD + HALF].astype(jnp.float32)
        second = ref[0, :, head * HD + HALF : (head + 1) * HD].astype(jnp.float32)
        cosine, sine = cos_ref[...], sin_ref[...]
        return (
            (first * cosine - second * sine).astype(jnp.bfloat16),
            (second * cosine + first * sine).astype(jnp.bfloat16),
        )

    def pack(head):
        first, second = turned(k_ref, head)
        kv[0, head, :, :HALF] = first
        kv[0, head, :, HALF:HD] = second
        kv[0, head, :, HD:] = v_ref[0, :, head * HD : (head + 1) * HD]

    pack(0)
    expected = jnp.where(me < seqs - 1, 1, 0) + (secs - 1 - sec)

    @pl.when(expected > 0)
    def _():
        pl.semaphore_wait(barrier, expected)

    @pl.when(me < seqs - 1)
    def _():
        kv_copy(0, 0).start()

    to_later(lambda target: gain_copy(sec, target).start())

    for head in range(1, HK):
        pack(head)
    for head in range(HQ):
        first, second = turned(q_ref, head)
        part = pl.ds((head % GROUP) * rows, rows)
        qrot[head // GROUP, part, :HALF] = first
        qrot[head // GROUP, part, HALF:] = second

    reach = jnp.minimum(place, float(WINDOW - 1)).astype(jnp.int32)
    gap = lax.broadcasted_iota(jnp.int32, (rows, rows), 0) - lax.broadcasted_iota(
        jnp.int32, (rows, rows), 1
    )
    for start in range(0, rows, HALF):
        low[:, start : start + HALF] = gap[:, start : start + HALF] - reach

    def block(step, head, first):
        for part in range(GROUP):
            at = pl.ds(part * rows, rows)
            score = lax.dot_general(
                qrot[head, at, :], kv[step, head, :, :HD], NT, preferred_element_type=jnp.float32
            )
            capped = jnp.tanh(score * (HD ** (-0.5) / 50.0))
            weight = jnp.exp2(capped * (50.0 * math.log2(math.e)))
            allowed = low[...] <= -step * rows
            if first:
                allowed = allowed & (gap >= 0)
            weight = jnp.where(allowed, weight, 0.0)
            total = weight[:, :HALF]
            for start in range(HALF, rows, HALF):
                total = total + weight[:, start : start + HALF]
            summed = lax.dot_general(
                weight.astype(jnp.bfloat16),
                kv[step, head, :, HD:],
                NN,
                preferred_element_type=jnp.float32,
            )
            if first:
                den[at, :] = total
                acc[at, :] = summed
            else:
                den[at, :] += total
                acc[at, :] += summed

    def one_head(head, carry):
        block(0, head, True)

        def earlier(step, carry):
            @pl.when((step == back) & (head < HK - 1) & (me < seqs - 1))
            def _():
                kv_copy(0, head + 1).start()

            @pl.when(me >= step)
            def _():
                kv_copy(step - 1, head).wait_recv()

                @pl.when((step < back) & (me < seqs - 1))
                def _():
                    kv_copy(step, head).start()

                block(step, head, False)

            return carry

        lax.fori_loop(1, back + 1, earlier, 0)
        for part in range(GROUP):
            at = pl.ds(part * rows, rows)
            cols = pl.ds(part * HD, HD)
            value = acc[at, :] / jnp.sum(den[at, :], axis=-1, keepdims=True)
            own[head, :, cols] = value
            sent[head, :, cols] = value.astype(jnp.bfloat16)
        to_later(lambda target: att_copy(sec, head, target).start())
        return carry

    lax.fori_loop(0, HK, one_head, 0)

    def norm_of(parts):
        square = 0.0
        for head in range(HK):
            value = parts(head)
            square = square + jnp.sum(value * value, axis=-1, keepdims=True)
        return lax.rsqrt(square * (1.0 / (HQ * HD)) + 1e-06)

    norm = norm_of(lambda head: own[head])
    for head in range(HK):
        cols = slice(head * PAIR, (head + 1) * PAIR)
        own[head] = own[head] * norm * gains[secs - 1, :1, cols] + res_ref[:, cols].astype(
            jnp.float32
        )

    for source in range(secs - 1):

        @pl.when(source < sec)
        def _(source=source):
            gain_copy(source, secs - 1).wait_recv()
            for head in range(HK):
                att_copy(source, head, secs - 1).wait_recv()
            norm = norm_of(lambda head: got[source, head].astype(jnp.float32))
            for head in range(HK):
                cols = slice(head * PAIR, (head + 1) * PAIR)
                own[head] += got[source, head].astype(jnp.float32) * norm * gains[source, :1, cols]

    for head in range(HK):
        out_ref[0, :, head * PAIR : (head + 1) * PAIR] = own[head].astype(jnp.bfloat16)

    def finish_head(head, carry):
        def finish_step(step, carry):
            @pl.when((me >= step) & (me < seqs - 1))
            def _():
                kv_copy(step, head).wait_send()

            return carry

        lax.fori_loop(0, back, finish_step, 0)
        to_later(lambda target: att_copy(sec, head, target).wait_send())
        return carry

    lax.fori_loop(0, HK, finish_head, 0)
    to_later(lambda target: gain_copy(sec, target).wait_send())


def per_device(queries, keys, values, segment_ids, positions, residual_in, post_gain):
    rows = positions.shape[0]
    seqs = lax.axis_size("seq")
    secs = lax.axis_size("section")
    longest = seqs * rows // 2
    back = min((min(WINDOW, longest) - 1 + rows - 1) // rows, seqs - 1)
    vmem = pl.BlockSpec(memory_space=pltpu.VMEM)
    return pl.pallas_call(
        functools.partial(kernel, seqs, secs, back, rows),
        out_shape=jax.ShapeDtypeStruct((1, rows, HQ * HD), jnp.bfloat16),
        in_specs=[vmem] * 6,
        out_specs=vmem,
        scratch_shapes=[
            pltpu.VMEM((back + 1, HK, rows, 2 * HD), jnp.bfloat16),
            pltpu.VMEM((HK, GROUP * rows, HD), jnp.bfloat16),
            pltpu.VMEM((rows, HALF), jnp.float32),
            pltpu.VMEM((rows, HALF), jnp.float32),
            pltpu.VMEM((rows, rows), jnp.int32),
            pltpu.VMEM((GROUP * rows, HD), jnp.float32),
            pltpu.VMEM((GROUP * rows, HALF), jnp.float32),
            pltpu.VMEM((HK, rows, PAIR), jnp.float32),
            pltpu.VMEM((HK, rows, PAIR), jnp.bfloat16),
            pltpu.VMEM((secs - 1, HK, rows, PAIR), jnp.bfloat16),
            pltpu.VMEM((secs, 8, HQ * HD), jnp.float32),
            pltpu.SemaphoreType.DMA((back, HK)),
            pltpu.SemaphoreType.DMA((back, HK)),
            pltpu.SemaphoreType.DMA((secs - 1, HK)),
            pltpu.SemaphoreType.DMA((secs - 1, HK)),
            pltpu.SemaphoreType.DMA((secs - 1,)),
            pltpu.SemaphoreType.DMA((secs - 1,)),
        ],
        compiler_params=pltpu.CompilerParams(
            collective_id=0, has_side_effects=True, vmem_limit_bytes=52 * 2**20
        ),
    )(queries, keys, values, positions.reshape(1, rows), residual_in, post_gain)


def solution(mesh):
    placed = (
        P("section", "seq", None),
        P("section", "seq", None),
        P("section", "seq", None),
        P("seq"),
        P("seq"),
        P("seq", None),
        P("section", None),
    )
    return jax.shard_map(
        per_device, mesh=mesh, in_specs=placed, out_specs=P("section", "seq", None), check_vma=False
    )
```

```python
import functools
import math

import jax
import jax.numpy as jnp
from jax import lax
from jax.experimental import pallas as pl
from jax.experimental.pallas import tpu as pltpu
from jax.sharding import PartitionSpec as P

HQ = 8
HK = 4
HD = 256
WINDOW = 4096
GROUP = HQ // HK
HALF = HD // 2
PAIR = GROUP * HD
MESH = pl.DeviceIdType.MESH
NT = (((1,), (1,)), ((), ()))
NN = (((1,), (0,)), ((), ()))


def kernel(
    seqs, secs, back, rows,
    q_ref, k_ref, v_ref, pos_ref, gain_ref,
    out_ref,
    q_in, k_in, pos_in, kv, qrot, cos_ref, sin_ref, low, acc, den, own, sent, got, square, gains,
    in_sem, v_sem, kv_send, kv_recv, att_send, att_recv, gain_send, gain_recv,
):
    me = lax.axis_index("seq")
    sec = lax.axis_index("section")

    barrier = pltpu.get_barrier_semaphore()

    @pl.when(me > 0)
    def _():
        pl.semaphore_signal(barrier, inc=1, device_id={"seq": me - 1}, device_id_type=MESH)

    for other in range(secs - 1):

        @pl.when(other < sec)
        def _(other=other):
            pl.semaphore_signal(barrier, inc=1, device_id={"section": other}, device_id_type=MESH)

    @pl.when(sec == 2)
    def _():
        pl.semaphore_signal(barrier, inc=1, device_id={"section": 3}, device_id_type=MESH)

    def columns(head):
        return pl.ds(head * HD, HD)

    pos_load = pltpu.make_async_copy(pos_ref, pos_in, in_sem.at[HK])
    q_load = pltpu.make_async_copy(q_ref, q_in, in_sem.at[HK + 1])
    gain_load = pltpu.make_async_copy(gain_ref, gains.at[secs - 1], in_sem.at[HK + 2])
    k_loads = [
        pltpu.make_async_copy(k_ref.at[0, :, columns(h)], k_in.at[h], in_sem.at[h])
        for h in range(HK)
    ]
    v_loads = [
        pltpu.make_async_copy(v_ref.at[0, :, columns(h)], kv.at[0, h, :, pl.ds(HD, HD)], v_sem.at[h])
        for h in range(HK)
    ]
    for load in [pos_load, k_loads[0], v_loads[0], gain_load, q_load] + k_loads[1:] + v_loads[1:]:
        load.start()

    def kv_copy(step, head):
        return pltpu.make_async_remote_copy(
            src_ref=kv.at[step, head],
            dst_ref=kv.at[step + 1, head],
            send_sem=kv_send.at[step, head],
            recv_sem=kv_recv.at[step, head],
            device_id={"seq": me + 1},
            device_id_type=MESH,
        )

    def own_copy(slot, source, piece, target):
        return pltpu.make_async_remote_copy(
            src_ref=sent.at[piece],
            dst_ref=got.at[source, piece],
            send_sem=att_send.at[slot, piece],
            recv_sem=att_recv.at[source, piece],
            device_id={"section": target},
            device_id_type=MESH,
        )

    def passed_copy(source, piece, target):
        return pltpu.make_async_remote_copy(
            src_ref=got.at[source, piece],
            dst_ref=got.at[source, piece],
            send_sem=att_send.at[1, piece],
            recv_sem=att_recv.at[source, piece],
            device_id={"section": target},
            device_id_type=MESH,
        )

    def gain_copy(source, target):
        return pltpu.make_async_remote_copy(
            src_ref=gains.at[secs - 1],
            dst_ref=gains.at[source],
            send_sem=gain_send.at[target - 1],
            recv_sem=gain_recv.at[source],
            device_id={"section": target},
            device_id_type=MESH,
        )

    def to_later(act):
        for target in range(1, secs):

            @pl.when(target > sec)
            def _(target=target):
                act(target)

    def send_piece(piece, act):
        @pl.when(sec == 0)
        def _():
            act(own_copy(0, 0, piece, 1))
            act(own_copy(1, 0, piece, 2))

        @pl.when(sec == 1)
        def _():
            act(own_copy(0, 1, piece, 3))

        @pl.when(sec == 2)
        def _():
            act(own_copy(0, 2, piece, 3))

    def pass_pieces(head, act):
        @pl.when(sec == 1)
        def _():
            act(passed_copy(0, GROUP * head, 3))

        @pl.when(sec == 2)
        def _():
            act(passed_copy(0, GROUP * head + 1, 3))

        @pl.when(sec == 3)
        def _():
            for part in range(GROUP):
                act(passed_copy(1, GROUP * head + part, 2))

    def arrive_and_go(copy):
        copy.wait_recv()
        copy.start()

    pos_load.wait()
    place = jnp.broadcast_to(pos_in[...], (HALF, rows)).astype(jnp.float32).T
    lane = lax.broadcasted_iota(jnp.int32, (rows, HALF), 1).astype(jnp.float32)
    angle = place * jnp.exp(lane * (-math.log(10000.0) / HALF))
    cos_ref[...] = jnp.cos(angle)
    sin_ref[...] = jnp.sin(angle)

    def turned(first, second):
        first, second = first.astype(jnp.float32), second.astype(jnp.float32)
        cosine, sine = cos_ref[...], sin_ref[...]
        return (
            (first * cosine - second * sine).astype(jnp.bfloat16),
            (second * cosine + first * sine).astype(jnp.bfloat16),
        )

    def pack(head):
        k_loads[head].wait()
        first, second = turned(k_in[head, :, :HALF], k_in[head, :, HALF:])
        kv[0, head, :, :HALF] = first
        kv[0, head, :, HALF:HD] = second
        v_loads[head].wait()

    pack(0)
    expected = (
        jnp.where(me < seqs - 1, 1, 0) + (secs - 1 - sec) + jnp.where(sec == 3, 1, 0)
    )

    @pl.when(expected > 0)
    def _():
        pl.semaphore_wait(barrier, expected)

    @pl.when(me < seqs - 1)
    def _():
        kv_copy(0, 0).start()

    gain_load.wait()
    to_later(lambda target: gain_copy(sec, target).start())

    q_load.wait()
    for head in range(HQ):
        at = head * HD
        first, second = turned(q_in[0, :, at : at + HALF], q_in[0, :, at + HALF : at + HD])
        part = pl.ds((head % GROUP) * rows, rows)
        qrot[head // GROUP, part, :HALF] = first
        qrot[head // GROUP, part, HALF:] = second
    for head in range(1, HK):
        pack(head)

    reach = jnp.minimum(place, float(WINDOW - 1)).astype(jnp.int32)
    gap = lax.broadcasted_iota(jnp.int32, (rows, rows), 0) - lax.broadcasted_iota(
        jnp.int32, (rows, rows), 1
    )
    for start in range(0, rows, HALF):
        low[:, start : start + HALF] = gap[:, start : start + HALF] - reach

    def block(step, head, first):
        for part in range(GROUP):
            at = pl.ds(part * rows, rows)
            score = lax.dot_general(
                qrot[head, at, :], kv[step, head, :, :HD], NT, preferred_element_type=jnp.float32
            )
            capped = jnp.tanh(score * (HD ** (-0.5) / 50.0))
            weight = jnp.exp2(capped * (50.0 * math.log2(math.e)))
            allowed = low[...] <= -step * rows
            if first:
                allowed = allowed & (gap >= 0)
            weight = jnp.where(allowed, weight, 0.0)
            total = weight[:, :HALF]
            for start in range(HALF, rows, HALF):
                total = total + weight[:, start : start + HALF]
            summed = lax.dot_general(
                weight.astype(jnp.bfloat16),
                kv[step, head, :, HD:],
                NN,
                preferred_element_type=jnp.float32,
            )
            if first:
                den[at, :] = total
                acc[at, :] = summed
            else:
                den[at, :] += total
                acc[at, :] += summed

    def one_head(head, carry):
        block(0, head, True)

        def earlier(step, carry):
            @pl.when((step == back) & (head < HK - 1) & (me < seqs - 1))
            def _():
                kv_copy(0, head + 1).start()

            @pl.when((step == back) & (head > 0))
            def _():
                pass_pieces(head - 1, arrive_and_go)

            @pl.when(me >= step)
            def _():
                kv_copy(step - 1, head).wait_recv()

                @pl.when((step < back) & (me < seqs - 1))
                def _():
                    kv_copy(step, head).start()

                block(step, head, False)

            return carry

        lax.fori_loop(1, back + 1, earlier, 0)
        for part in range(GROUP):
            at = pl.ds(part * rows, rows)
            value = acc[at, :] / jnp.sum(den[at, :], axis=-1, keepdims=True)
            own[GROUP * head + part] = value
            sent[GROUP * head + part] = value.astype(jnp.bfloat16)
            send_piece(GROUP * head + part, lambda copy: copy.start())
        return carry

    lax.fori_loop(0, HK, one_head, 0)

    def squares(parts, pieces):
        total = 0.0
        for piece in pieces:
            value = parts[piece].astype(jnp.float32)
            value = value * value
            for start in range(0, HD, HALF):
                total = total + value[:, start : start + HALF]
        return total

    def norm_of(total):
        return lax.rsqrt(
            jnp.sum(total, axis=-1, keepdims=True) * (1.0 / (HQ * HD)) + 1e-06
        )

    norm = norm_of(squares(own, range(HQ)))
    for piece in range(HQ):
        own[piece] = own[piece] * norm * gains[secs - 1, :, piece * HD : (piece + 1) * HD]

    def wait_piece(source, piece):
        passed = (
            ((sec == 1) & (source == 0) & (piece % GROUP == 0))
            | ((sec == 2) & (source == 0) & (piece % GROUP == 1))
            | ((sec == 3) & (source == 1))
        )

        @pl.when(jnp.logical_not(passed))
        def _():
            passed_copy(source, piece, 3).wait_recv()

    late = range(HQ - GROUP, HQ)
    early = range(HQ - GROUP)
    for source in range(secs - 1):

        @pl.when(source < sec)
        def _(source=source):
            gain_copy(source, secs - 1).wait_recv()
            for piece in early:
                wait_piece(source, piece)
            square[source] = squares(got.at[source], early)

    pass_pieces(HK - 1, arrive_and_go)
    for source in range(secs - 1):

        @pl.when(source < sec)
        def _(source=source):
            for piece in late:
                wait_piece(source, piece)

    for layer in range(secs):

        @pl.when(sec == layer)
        def _(layer=layer):
            norms = [norm_of(square[k] + squares(got.at[k], late)) for k in range(layer)]
            for piece in range(HQ):
                cols = slice(piece * HD, (piece + 1) * HD)
                total = own[piece]
                for k in range(layer):
                    total = total + got[k, piece].astype(jnp.float32) * norms[k] * gains[k, :, cols]
                out_ref[0, :, cols] = total.astype(jnp.bfloat16)

    def finish_head(head, carry):
        def finish_step(step, carry):
            @pl.when((me >= step) & (me < seqs - 1))
            def _():
                kv_copy(step, head).wait_send()

            return carry

        lax.fori_loop(0, back, finish_step, 0)
        for part in range(GROUP):
            send_piece(GROUP * head + part, lambda copy: copy.wait_send())
        pass_pieces(head, lambda copy: copy.wait_send())
        return carry

    lax.fori_loop(0, HK, finish_head, 0)
    to_later(lambda target: gain_copy(sec, target).wait_send())


def per_device(queries, keys, values, segment_ids, positions, residual_in, post_gain):
    rows = positions.shape[0]
    seqs = lax.axis_size("seq")
    secs = lax.axis_size("section")
    longest = seqs * rows // 2
    back = min((min(WINDOW, longest) - 1 + rows - 1) // rows, seqs - 1)
    hbm = pl.BlockSpec(memory_space=pl.ANY)
    vmem = pl.BlockSpec(memory_space=pltpu.VMEM)
    summed = pl.pallas_call(
        functools.partial(kernel, seqs, secs, back, rows),
        out_shape=jax.ShapeDtypeStruct((1, rows, HQ * HD), jnp.bfloat16),
        in_specs=[hbm] * 5,
        out_specs=vmem,
        scratch_shapes=[
            pltpu.VMEM((1, rows, HQ * HD), jnp.bfloat16),
            pltpu.VMEM((HK, rows, HD), jnp.bfloat16),
            pltpu.VMEM((1, rows), jnp.int32),
            pltpu.VMEM((back + 1, HK, rows, 2 * HD), jnp.bfloat16),
            pltpu.VMEM((HK, GROUP * rows, HD), jnp.bfloat16),
            pltpu.VMEM((rows, HALF), jnp.float32),
            pltpu.VMEM((rows, HALF), jnp.float32),
            pltpu.VMEM((rows, rows), jnp.int32),
            pltpu.VMEM((GROUP * rows, HD), jnp.float32),
            pltpu.VMEM((GROUP * rows, HALF), jnp.float32),
            pltpu.VMEM((HQ, rows, HD), jnp.float32),
            pltpu.VMEM((HQ, rows, HD), jnp.bfloat16),
            pltpu.VMEM((secs - 1, HQ, rows, HD), jnp.bfloat16),
            pltpu.VMEM((secs - 1, rows, HALF), jnp.float32),
            pltpu.VMEM((secs, 1, HQ * HD), jnp.float32),
            pltpu.SemaphoreType.DMA((HK + 3,)),
            pltpu.SemaphoreType.DMA((HK,)),
            pltpu.SemaphoreType.DMA((back, HK)),
            pltpu.SemaphoreType.DMA((back, HK)),
            pltpu.SemaphoreType.DMA((2, HQ)),
            pltpu.SemaphoreType.DMA((secs - 1, HQ)),
            pltpu.SemaphoreType.DMA((secs - 1,)),
            pltpu.SemaphoreType.DMA((secs - 1,)),
        ],
        compiler_params=pltpu.CompilerParams(
            collective_id=0, has_side_effects=True, vmem_limit_bytes=52 * 2**20
        ),
    )(queries, keys, values, positions.reshape(1, rows), post_gain)
    running = summed.astype(jnp.float32) + residual_in.astype(jnp.float32)[None]
    return running.astype(jnp.bfloat16)


def solution(mesh):
    placed = (
        P("section", "seq", None),
        P("section", "seq", None),
        P("section", "seq", None),
        P("seq"),
        P("seq"),
        P("seq", None),
        P("section", None),
    )
    return jax.shard_map(
        per_device, mesh=mesh, in_specs=placed, out_specs=P("section", "seq", None), check_vma=False
    )
```

```python
import functools
import math

import jax
import jax.numpy as jnp
from jax import lax
from jax.experimental import pallas as pl
from jax.experimental.pallas import tpu as pltpu
from jax.sharding import PartitionSpec as P

HQ = 8
HK = 4
HD = 256
WINDOW = 4096
GROUP = HQ // HK
HALF = HD // 2
PAIR = GROUP * HD
MESH = pl.DeviceIdType.MESH
NT = (((1,), (1,)), ((), ()))
NN = (((1,), (0,)), ((), ()))


def kernel(
    seqs, secs, back, rows,
    q_ref, k_ref, v_ref, pos_ref, gain_ref,
    out_ref,
    q_in, k_in, pos_in, kv, qrot, cos_ref, sin_ref, low, acc, den, late_w, own, sent, got, square,
    norms, gains,
    in_sem, v_sem, kv_send, kv_recv, att_send, att_recv, gain_send, gain_recv, norm_send, norm_recv,
):
    me = lax.axis_index("seq")
    sec = lax.axis_index("section")

    barrier = pltpu.get_barrier_semaphore()

    @pl.when(me > 0)
    def _():
        pl.semaphore_signal(barrier, inc=1, device_id={"seq": me - 1}, device_id_type=MESH)

    for other in range(secs - 1):

        @pl.when(other < sec)
        def _(other=other):
            pl.semaphore_signal(barrier, inc=1, device_id={"section": other}, device_id_type=MESH)

    @pl.when(sec == 2)
    def _():
        pl.semaphore_signal(barrier, inc=1, device_id={"section": 3}, device_id_type=MESH)

    def columns(head):
        return pl.ds(head * HD, HD)

    pos_load = pltpu.make_async_copy(pos_ref, pos_in, in_sem.at[HK])
    q_load = pltpu.make_async_copy(q_ref, q_in, in_sem.at[HK + 1])
    gain_load = pltpu.make_async_copy(gain_ref, gains.at[secs - 1], in_sem.at[HK + 2])
    k_loads = [
        pltpu.make_async_copy(k_ref.at[0, :, columns(h)], k_in.at[h], in_sem.at[h])
        for h in range(HK)
    ]
    v_loads = [
        pltpu.make_async_copy(v_ref.at[0, :, columns(h)], kv.at[0, h, :, pl.ds(HD, HD)], v_sem.at[h])
        for h in range(HK)
    ]
    for load in [pos_load, k_loads[0], v_loads[0], gain_load, q_load] + k_loads[1:] + v_loads[1:]:
        load.start()

    def kv_copy(step, chunk):
        if not isinstance(chunk, int) or chunk < HK - 1:
            at = lambda block: kv.at[block, chunk]
        elif chunk == HK - 1:
            at = lambda block: kv.at[block, HK - 1, :, pl.ds(0, HD + HALF)]
        else:
            at = lambda block: kv.at[block, HK - 1, :, pl.ds(HD + HALF, HALF)]
        return pltpu.make_async_remote_copy(
            src_ref=at(step),
            dst_ref=at(step + 1),
            send_sem=kv_send.at[step, chunk],
            recv_sem=kv_recv.at[step, chunk],
            device_id={"seq": me + 1},
            device_id_type=MESH,
        )

    def piece_of(ref, piece):
        if not isinstance(piece, int) or piece < HQ - GROUP:
            return ref.at[piece]
        late = piece - (HQ - GROUP)
        return ref.at[HQ - GROUP + late % GROUP, late // GROUP]

    def own_copy(slot, source, piece, target):
        return pltpu.make_async_remote_copy(
            src_ref=piece_of(sent, piece),
            dst_ref=piece_of(got.at[source], piece),
            send_sem=att_send.at[slot, piece],
            recv_sem=att_recv.at[source, piece],
            device_id={"section": target},
            device_id_type=MESH,
        )

    def passed_copy(source, piece, target):
        return pltpu.make_async_remote_copy(
            src_ref=piece_of(got.at[source], piece),
            dst_ref=piece_of(got.at[source], piece),
            send_sem=att_send.at[1, piece],
            recv_sem=att_recv.at[source, piece],
            device_id={"section": target},
            device_id_type=MESH,
        )

    def gain_copy(source, target):
        return pltpu.make_async_remote_copy(
            src_ref=gains.at[secs - 1],
            dst_ref=gains.at[source],
            send_sem=gain_send.at[target - 1],
            recv_sem=gain_recv.at[source],
            device_id={"section": target},
            device_id_type=MESH,
        )

    def norm_copy(source, target):
        return pltpu.make_async_remote_copy(
            src_ref=norms.at[secs - 1],
            dst_ref=norms.at[source],
            send_sem=norm_send.at[target - 1],
            recv_sem=norm_recv.at[source],
            device_id={"section": target},
            device_id_type=MESH,
        )

    def to_later(act):
        for target in range(1, secs):

            @pl.when(target > sec)
            def _(target=target):
                act(target)

    def send_piece(piece, act):
        @pl.when(sec == 0)
        def _():
            act(own_copy(0, 0, piece, 1))
            act(own_copy(1, 0, piece, 2))

        @pl.when(sec == 1)
        def _():
            act(own_copy(0, 1, piece, 3))

        @pl.when(sec == 2)
        def _():
            act(own_copy(0, 2, piece, 3))

    def pass_pieces(head, act):
        @pl.when(sec == 1)
        def _():
            act(passed_copy(0, GROUP * head, 3))

        @pl.when(sec == 2)
        def _():
            act(passed_copy(0, GROUP * head + 1, 3))

        @pl.when(sec == 3)
        def _():
            for part in range(GROUP):
                act(passed_copy(1, GROUP * head + part, 2))

    def arrive_and_go(copy):
        copy.wait_recv()
        copy.start()

    pos_load.wait()
    place = jnp.broadcast_to(pos_in[...], (HALF, rows)).astype(jnp.float32).T
    lane = lax.broadcasted_iota(jnp.int32, (rows, HALF), 1).astype(jnp.float32)
    angle = place * jnp.exp(lane * (-math.log(10000.0) / HALF))
    cos_ref[...] = jnp.cos(angle)
    sin_ref[...] = jnp.sin(angle)

    def turned(first, second):
        first, second = first.astype(jnp.float32), second.astype(jnp.float32)
        cosine, sine = cos_ref[...], sin_ref[...]
        return (
            (first * cosine - second * sine).astype(jnp.bfloat16),
            (second * cosine + first * sine).astype(jnp.bfloat16),
        )

    def pack(head):
        k_loads[head].wait()
        first, second = turned(k_in[head, :, :HALF], k_in[head, :, HALF:])
        kv[0, head, :, :HALF] = first
        kv[0, head, :, HALF:HD] = second
        v_loads[head].wait()

    pack(0)
    expected = (
        jnp.where(me < seqs - 1, 1, 0) + (secs - 1 - sec) + jnp.where(sec == 3, 1, 0)
    )

    @pl.when(expected > 0)
    def _():
        pl.semaphore_wait(barrier, expected)

    @pl.when(me < seqs - 1)
    def _():
        kv_copy(0, 0).start()

    gain_load.wait()
    to_later(lambda target: gain_copy(sec, target).start())

    q_load.wait()
    for head in range(HQ):
        at = head * HD
        first, second = turned(q_in[0, :, at : at + HALF], q_in[0, :, at + HALF : at + HD])
        part = pl.ds((head % GROUP) * rows, rows)
        qrot[head // GROUP, part, :HALF] = first
        qrot[head // GROUP, part, HALF:] = second
    for head in range(1, HK):
        pack(head)

    reach = jnp.minimum(place, float(WINDOW - 1)).astype(jnp.int32)
    gap = lax.broadcasted_iota(jnp.int32, (rows, rows), 0) - lax.broadcasted_iota(
        jnp.int32, (rows, rows), 1
    )
    for start in range(0, rows, HALF):
        low[:, start : start + HALF] = gap[:, start : start + HALF] - reach

    def weights(step, head, part, first):
        at = pl.ds(part * rows, rows)
        score = lax.dot_general(
            qrot[head, at, :], kv[step, head, :, :HD], NT, preferred_element_type=jnp.float32
        )
        capped = jnp.tanh(score * (HD ** (-0.5) / 50.0))
        weight = jnp.exp2(capped * (50.0 * math.log2(math.e)))
        allowed = low[...] <= -step * rows
        if first:
            allowed = allowed & (gap >= 0)
        weight = jnp.where(allowed, weight, 0.0)
        total = weight[:, :HALF]
        for start in range(HALF, rows, HALF):
            total = total + weight[:, start : start + HALF]
        if first:
            den[at, :] = total
        else:
            den[at, :] += total
        return weight.astype(jnp.bfloat16)

    def add_values(weight, step, head, part, cols, first):
        at = pl.ds(part * rows, rows)
        summed = lax.dot_general(
            weight,
            kv[step, head, :, HD + cols.start : HD + cols.stop],
            NN,
            preferred_element_type=jnp.float32,
        )
        if first:
            acc[at, cols] = summed
        else:
            acc[at, cols] += summed

    def block(step, head, first):
        for part in range(GROUP):
            weight = weights(step, head, part, first)
            add_values(weight, step, head, part, slice(0, HD), first)

    def block_keep(step, first):
        for part in range(GROUP):
            weight = weights(step, HK - 1, part, first)
            late_w[step, part] = weight
            add_values(weight, step, HK - 1, part, slice(0, HALF), first)

    def block_kept(step, first):
        for part in range(GROUP):
            add_values(late_w[step, part], step, HK - 1, part, slice(HALF, HD), first)

    def start_own(chunk):
        @pl.when(me < seqs - 1)
        def _():
            kv_copy(0, chunk).start()

    def stream(chunk, work, last, passing):
        def earlier(step, carry):
            @pl.when(step == back)
            def _():
                last()

            @pl.when(me >= step)
            def _():
                kv_copy(step - 1, chunk).wait_recv()

                @pl.when((step < back) & (me < seqs - 1))
                def _():
                    kv_copy(step, chunk).start()

                work(step)

            @pl.when(step == max(back - 1, 1))
            def _():
                passing()

            return carry

        lax.fori_loop(1, back + 1, earlier, 0)

    def finish_piece(piece, part, halves):
        at = pl.ds(part * rows, rows)
        share = 1.0 / jnp.sum(den[at, :], axis=-1, keepdims=True)
        total = 0.0
        for half in halves:
            value = acc[at, half * HALF : (half + 1) * HALF] * share
            own[piece, half] = value
            sent[piece, half] = value.astype(jnp.bfloat16)
            total = total + value * value
        square[...] += total

    square[...] = jnp.zeros_like(square)

    def one_head(head, carry):
        def last():
            @pl.when(head < HK - 2)
            def _():
                start_own(head + 1)

            @pl.when(head == HK - 2)
            def _():
                start_own(HK - 1)

        def passing():
            @pl.when(head > 0)
            def _():
                pass_pieces(head - 1, arrive_and_go)

        block(0, head, True)
        stream(head, lambda step: block(step, head, False), last, passing)
        for part in range(GROUP):
            finish_piece(GROUP * head + part, part, (0, 1))
            send_piece(GROUP * head + part, lambda copy: copy.start())
        return carry

    lax.fori_loop(0, HK - 1, one_head, 0)

    block_keep(0, True)
    stream(
        HK - 1,
        lambda step: block_keep(step, False),
        lambda: start_own(HK),
        lambda: pass_pieces(HK - 2, arrive_and_go),
    )
    for part in range(GROUP):
        finish_piece(HQ - GROUP + part, part, (0,))
        send_piece(HQ - GROUP + part, lambda copy: copy.start())
    block_kept(0, True)
    stream(HK, lambda step: block_kept(step, False), lambda: None, lambda: None)
    for part in range(GROUP):
        finish_piece(HQ - GROUP + part, part, (1,))
        send_piece(HQ + part, lambda copy: copy.start())

    mean = jnp.sum(square[...], axis=-1, keepdims=True) * (1.0 / (HQ * HD))
    norm = jnp.broadcast_to(lax.rsqrt(mean + 1e-06), (rows, HALF))
    norms[secs - 1] = norm.T[:1, :]
    to_later(lambda target: norm_copy(sec, target).start())
    square[...] = norm

    pass_pieces(HK - 1, arrive_and_go)
    pass_pieces(HK, arrive_and_go)

    def wait_piece(source, piece):
        passed = (
            ((sec == 1) & (source == 0) & (piece % GROUP == 0))
            | ((sec == 2) & (source == 0) & (piece % GROUP == 1))
            | ((sec == 3) & (source == 1))
        )

        @pl.when(jnp.logical_not(passed))
        def _():
            passed_copy(source, piece, 3).wait_recv()

    def wait_pieces(pieces):
        for source in range(secs - 1):

            @pl.when(source < sec)
            def _(source=source):
                for piece in pieces:
                    wait_piece(source, piece)

    def add_layers(places):
        for layer in range(secs):

            @pl.when(sec == layer)
            def _(layer=layer):
                spread = [
                    jnp.broadcast_to(norms[k], (HALF, rows)).T for k in range(layer)
                ]
                for head, half in places:
                    cols = slice(head * HD + half * HALF, head * HD + (half + 1) * HALF)
                    total = own[head, half] * square[...] * gains[secs - 1, :, cols]
                    for k in range(layer):
                        part = got[k, head, half].astype(jnp.float32)
                        total = total + part * spread[k] * gains[k, :, cols]
                    out_ref[0, :, cols] = total.astype(jnp.bfloat16)

    for source in range(secs - 1):

        @pl.when(source < sec)
        def _(source=source):
            gain_copy(source, secs - 1).wait_recv()
            norm_copy(source, secs - 1).wait_recv()

    early, late = range(HQ - GROUP), range(HQ - GROUP, HQ)
    wait_pieces(early)
    add_layers([(head, half) for head in early for half in (0, 1)])
    for half in (0, 1):
        wait_pieces(range(HQ - GROUP + half * GROUP, HQ + half * GROUP))
        add_layers([(head, half) for head in late])

    def finish(chunk):
        def finish_step(step, carry):
            @pl.when((me >= step) & (me < seqs - 1))
            def _():
                kv_copy(step, chunk).wait_send()

            return carry

        lax.fori_loop(0, back, finish_step, 0)
        for part in range(GROUP):
            send_piece(GROUP * chunk + part, lambda copy: copy.wait_send())
        pass_pieces(chunk, lambda copy: copy.wait_send())

    def finish_head(head, carry):
        finish(head)
        return carry

    lax.fori_loop(0, HK - 1, finish_head, 0)
    finish(HK - 1)
    finish(HK)
    to_later(lambda target: gain_copy(sec, target).wait_send())
    to_later(lambda target: norm_copy(sec, target).wait_send())


def per_device(queries, keys, values, segment_ids, positions, residual_in, post_gain):
    rows = positions.shape[0]
    seqs = lax.axis_size("seq")
    secs = lax.axis_size("section")
    longest = seqs * rows // 2
    back = min((min(WINDOW, longest) - 1 + rows - 1) // rows, seqs - 1)
    hbm = pl.BlockSpec(memory_space=pltpu.HBM)
    vmem = pl.BlockSpec(memory_space=pltpu.VMEM)
    summed = pl.pallas_call(
        functools.partial(kernel, seqs, secs, back, rows),
        out_shape=pltpu.VMEM((1, rows, HQ * HD), jnp.bfloat16),
        in_specs=[hbm] * 5,
        out_specs=vmem,
        scratch_shapes=[
            pltpu.VMEM((1, rows, HQ * HD), jnp.bfloat16),
            pltpu.VMEM((HK, rows, HD), jnp.bfloat16),
            pltpu.VMEM((1, rows), jnp.int32),
            pltpu.VMEM((back + 1, HK, rows, 2 * HD), jnp.bfloat16),
            pltpu.VMEM((HK, GROUP * rows, HD), jnp.bfloat16),
            pltpu.VMEM((rows, HALF), jnp.float32),
            pltpu.VMEM((rows, HALF), jnp.float32),
            pltpu.VMEM((rows, rows), jnp.int32),
            pltpu.VMEM((GROUP * rows, HD), jnp.float32),
            pltpu.VMEM((GROUP * rows, HALF), jnp.float32),
            pltpu.VMEM((back + 1, GROUP, rows, rows), jnp.bfloat16),
            pltpu.VMEM((HQ, 2, rows, HALF), jnp.float32),
            pltpu.VMEM((HQ, 2, rows, HALF), jnp.bfloat16),
            pltpu.VMEM((secs - 1, HQ, 2, rows, HALF), jnp.bfloat16),
            pltpu.VMEM((rows, HALF), jnp.float32),
            pltpu.VMEM((secs, 1, rows), jnp.float32),
            pltpu.VMEM((secs, 1, HQ * HD), jnp.float32),
            pltpu.SemaphoreType.DMA((HK + 3,)),
            pltpu.SemaphoreType.DMA((HK,)),
            pltpu.SemaphoreType.DMA((back, HK + 1)),
            pltpu.SemaphoreType.DMA((back, HK + 1)),
            pltpu.SemaphoreType.DMA((2, HQ + GROUP)),
            pltpu.SemaphoreType.DMA((secs - 1, HQ + GROUP)),
            pltpu.SemaphoreType.DMA((secs - 1,)),
            pltpu.SemaphoreType.DMA((secs - 1,)),
            pltpu.SemaphoreType.DMA((secs - 1,)),
            pltpu.SemaphoreType.DMA((secs - 1,)),
        ],
        compiler_params=pltpu.CompilerParams(
            collective_id=0, has_side_effects=True, vmem_limit_bytes=60 * 2**20
        ),
    )(queries, keys, values, positions.reshape(1, rows), post_gain)
    running = summed.astype(jnp.float32) + residual_in.astype(jnp.float32)[None]
    return running.astype(jnp.bfloat16)


def solution(mesh):
    placed = (
        P("section", "seq", None),
        P("section", "seq", None),
        P("section", "seq", None),
        P("seq"),
        P("seq"),
        P("seq", None),
        P("section", None),
    )
    return jax.shard_map(
        per_device, mesh=mesh, in_specs=placed, out_specs=P("section", "seq", None), check_vma=False
    )
```

```python
import functools
import math

import jax
import jax.numpy as jnp
from jax import lax
from jax.experimental import pallas as pl
from jax.experimental.pallas import tpu as pltpu
from jax.sharding import PartitionSpec as P

HQ = 8
HK = 4
HD = 256
WINDOW = 4096
GROUP = HQ // HK
HALF = HD // 2
PAIR = GROUP * HD
MESH = pl.DeviceIdType.MESH
NT = (((1,), (1,)), ((), ()))
NN = (((1,), (0,)), ((), ()))


def kernel(
    seqs, secs, back, rows,
    q_ref, k_ref, v_ref, pos_ref, gain_ref,
    out_ref,
    q_in, k_in, pos_in, kv, qrot, cos_ref, sin_ref, low, acc, den, late_w, own, sent, got, square,
    norms, gains,
    in_sem, v_sem, kv_send, kv_recv, att_send, att_recv, gain_send, gain_recv, norm_send, norm_recv,
):
    me = lax.axis_index("seq")
    sec = lax.axis_index("section")

    even = lax.rem(me, 2) == 0
    barrier = pltpu.get_barrier_semaphore()

    @pl.when(me > 0)
    def _():
        pl.semaphore_signal(barrier, inc=1, device_id={"seq": me - 1}, device_id_type=MESH)

    @pl.when(even & (me > 1))
    def _():
        pl.semaphore_signal(barrier, inc=1, device_id={"seq": me - 2}, device_id_type=MESH)

    for other in range(secs - 1):

        @pl.when(other < sec)
        def _(other=other):
            pl.semaphore_signal(barrier, inc=1, device_id={"section": other}, device_id_type=MESH)

    @pl.when(sec == 2)
    def _():
        pl.semaphore_signal(barrier, inc=1, device_id={"section": 3}, device_id_type=MESH)

    def columns(head):
        return pl.ds(head * HD, HD)

    pos_load = pltpu.make_async_copy(pos_ref, pos_in, in_sem.at[HK])
    q_load = pltpu.make_async_copy(q_ref, q_in, in_sem.at[HK + 1])
    gain_load = pltpu.make_async_copy(gain_ref, gains.at[secs - 1], in_sem.at[HK + 2])
    k_loads = [
        pltpu.make_async_copy(k_ref.at[0, :, columns(h)], k_in.at[h], in_sem.at[h])
        for h in range(HK)
    ]
    v_loads = [
        pltpu.make_async_copy(v_ref.at[0, :, columns(h)], kv.at[0, h, :, pl.ds(HD, HD)], v_sem.at[h])
        for h in range(HK)
    ]
    for load in [pos_load, k_loads[0], v_loads[0], gain_load, q_load] + k_loads[1:] + v_loads[1:]:
        load.start()

    def kv_copy(step, chunk, by=1):
        if not isinstance(chunk, int) or chunk < HK - 1:
            at = lambda block: kv.at[block, chunk]
        elif chunk == HK - 1:
            at = lambda block: kv.at[block, HK - 1, :, pl.ds(0, HD + HALF)]
        else:
            at = lambda block: kv.at[block, HK - 1, :, pl.ds(HD + HALF, HALF)]
        return pltpu.make_async_remote_copy(
            src_ref=at(step),
            dst_ref=at(step + by),
            send_sem=kv_send.at[by - 1, step, chunk],
            recv_sem=kv_recv.at[step + by - 1, chunk],
            device_id={"seq": me + by},
            device_id_type=MESH,
        )

    def send_block(step, chunk, act):
        @pl.when(even & (me + 2 < seqs) & (step + 2 <= back))
        def _():
            act(kv_copy(step, chunk, 2))

        @pl.when((even | (step == 0)) & (me + 1 < seqs) & (step + 1 <= back))
        def _():
            act(kv_copy(step, chunk, 1))

    def piece_of(ref, piece):
        if not isinstance(piece, int) or piece < HQ - GROUP:
            return ref.at[piece]
        late = piece - (HQ - GROUP)
        return ref.at[HQ - GROUP + late % GROUP, late // GROUP]

    def own_copy(slot, source, piece, target):
        return pltpu.make_async_remote_copy(
            src_ref=piece_of(sent, piece),
            dst_ref=piece_of(got.at[source], piece),
            send_sem=att_send.at[slot, piece],
            recv_sem=att_recv.at[source, piece],
            device_id={"section": target},
            device_id_type=MESH,
        )

    def passed_copy(source, piece, target):
        return pltpu.make_async_remote_copy(
            src_ref=piece_of(got.at[source], piece),
            dst_ref=piece_of(got.at[source], piece),
            send_sem=att_send.at[1, piece],
            recv_sem=att_recv.at[source, piece],
            device_id={"section": target},
            device_id_type=MESH,
        )

    def gain_copy(source, target):
        return pltpu.make_async_remote_copy(
            src_ref=gains.at[secs - 1],
            dst_ref=gains.at[source],
            send_sem=gain_send.at[target - 1],
            recv_sem=gain_recv.at[source],
            device_id={"section": target},
            device_id_type=MESH,
        )

    def norm_copy(source, target):
        return pltpu.make_async_remote_copy(
            src_ref=norms.at[secs - 1],
            dst_ref=norms.at[source],
            send_sem=norm_send.at[target - 1],
            recv_sem=norm_recv.at[source],
            device_id={"section": target},
            device_id_type=MESH,
        )

    def to_later(act):
        for target in range(1, secs):

            @pl.when(target > sec)
            def _(target=target):
                act(target)

    def send_piece(piece, act):
        @pl.when(sec == 0)
        def _():
            act(own_copy(0, 0, piece, 1))
            act(own_copy(1, 0, piece, 2))

        @pl.when(sec == 1)
        def _():
            act(own_copy(0, 1, piece, 3))

        @pl.when(sec == 2)
        def _():
            act(own_copy(0, 2, piece, 3))

    def pass_pieces(head, act):
        @pl.when(sec == 1)
        def _():
            act(passed_copy(0, GROUP * head, 3))

        @pl.when(sec == 2)
        def _():
            act(passed_copy(0, GROUP * head + 1, 3))

        @pl.when(sec == 3)
        def _():
            for part in range(GROUP):
                act(passed_copy(1, GROUP * head + part, 2))

    def arrive_and_go(copy):
        copy.wait_recv()
        copy.start()

    pos_load.wait()
    place = jnp.broadcast_to(pos_in[...], (HALF, rows)).astype(jnp.float32).T
    lane = lax.broadcasted_iota(jnp.int32, (rows, HALF), 1).astype(jnp.float32)
    angle = place * jnp.exp(lane * (-math.log(10000.0) / HALF))
    cos_ref[...] = jnp.cos(angle)
    sin_ref[...] = jnp.sin(angle)

    def turned(first, second):
        first, second = first.astype(jnp.float32), second.astype(jnp.float32)
        cosine, sine = cos_ref[...], sin_ref[...]
        return (
            (first * cosine - second * sine).astype(jnp.bfloat16),
            (second * cosine + first * sine).astype(jnp.bfloat16),
        )

    def pack(head):
        k_loads[head].wait()
        first, second = turned(k_in[head, :, :HALF], k_in[head, :, HALF:])
        kv[0, head, :, :HALF] = first
        kv[0, head, :, HALF:HD] = second
        v_loads[head].wait()

    pack(0)
    expected = (
        jnp.where(me < seqs - 1, 1, 0)
        + jnp.where(even & (me + 2 < seqs), 1, 0)
        + (secs - 1 - sec)
        + jnp.where(sec == 3, 1, 0)
    )

    @pl.when(expected > 0)
    def _():
        pl.semaphore_wait(barrier, expected)

    send_block(0, 0, lambda copy: copy.start())

    gain_load.wait()
    to_later(lambda target: gain_copy(sec, target).start())

    q_load.wait()
    for head in range(HQ):
        at = head * HD
        first, second = turned(q_in[0, :, at : at + HALF], q_in[0, :, at + HALF : at + HD])
        part = pl.ds((head % GROUP) * rows, rows)
        qrot[head // GROUP, part, :HALF] = first
        qrot[head // GROUP, part, HALF:] = second
    for head in range(1, HK):
        pack(head)

    reach = jnp.minimum(place, float(WINDOW - 1)).astype(jnp.int32)
    gap = lax.broadcasted_iota(jnp.int32, (rows, rows), 0) - lax.broadcasted_iota(
        jnp.int32, (rows, rows), 1
    )
    for start in range(0, rows, HALF):
        low[:, start : start + HALF] = gap[:, start : start + HALF] - reach

    def weights(step, head, part, first):
        at = pl.ds(part * rows, rows)
        score = lax.dot_general(
            qrot[head, at, :], kv[step, head, :, :HD], NT, preferred_element_type=jnp.float32
        )
        capped = jnp.tanh(score * (HD ** (-0.5) / 50.0))
        weight = jnp.exp2(capped * (50.0 * math.log2(math.e)))
        allowed = low[...] <= -step * rows
        if first:
            allowed = allowed & (gap >= 0)
        weight = jnp.where(allowed, weight, 0.0)
        total = weight[:, :HALF]
        for start in range(HALF, rows, HALF):
            total = total + weight[:, start : start + HALF]
        if first:
            den[at, :] = total
        else:
            den[at, :] += total
        return weight.astype(jnp.bfloat16)

    def add_values(weight, step, head, part, cols, first):
        at = pl.ds(part * rows, rows)
        summed = lax.dot_general(
            weight,
            kv[step, head, :, HD + cols.start : HD + cols.stop],
            NN,
            preferred_element_type=jnp.float32,
        )
        if first:
            acc[at, cols] = summed
        else:
            acc[at, cols] += summed

    def block(step, head, first):
        for part in range(GROUP):
            weight = weights(step, head, part, first)
            add_values(weight, step, head, part, slice(0, HD), first)

    def block_keep(step, first):
        for part in range(GROUP):
            weight = weights(step, HK - 1, part, first)
            late_w[step, part] = weight
            add_values(weight, step, HK - 1, part, slice(0, HALF), first)

    def block_kept(step, first):
        for part in range(GROUP):
            add_values(late_w[step, part], step, HK - 1, part, slice(HALF, HD), first)

    def start_own(chunk):
        send_block(0, chunk, lambda copy: copy.start())

    def stream(chunk, work, last, passing):
        def earlier(step, carry):
            @pl.when(step == back)
            def _():
                last()

            @pl.when(me >= step)
            def _():
                kv_copy(step - 1, chunk).wait_recv()

                send_block(step, chunk, lambda copy: copy.start())
                work(step)

            @pl.when(step == max(back - 1, 1))
            def _():
                passing()

            return carry

        lax.fori_loop(1, back + 1, earlier, 0)

    def finish_piece(piece, part, halves):
        at = pl.ds(part * rows, rows)
        share = 1.0 / jnp.sum(den[at, :], axis=-1, keepdims=True)
        total = 0.0
        for half in halves:
            value = acc[at, half * HALF : (half + 1) * HALF] * share
            own[piece, half] = value
            sent[piece, half] = value.astype(jnp.bfloat16)
            total = total + value * value
        square[...] += total

    square[...] = jnp.zeros_like(square)

    def one_head(head, carry):
        def last():
            @pl.when(head < HK - 2)
            def _():
                start_own(head + 1)

            @pl.when(head == HK - 2)
            def _():
                start_own(HK - 1)

        def passing():
            @pl.when(head > 0)
            def _():
                pass_pieces(head - 1, arrive_and_go)

        block(0, head, True)
        stream(head, lambda step: block(step, head, False), last, passing)
        for part in range(GROUP):
            finish_piece(GROUP * head + part, part, (0, 1))
            send_piece(GROUP * head + part, lambda copy: copy.start())
        return carry

    lax.fori_loop(0, HK - 1, one_head, 0)

    block_keep(0, True)
    stream(
        HK - 1,
        lambda step: block_keep(step, False),
        lambda: start_own(HK),
        lambda: pass_pieces(HK - 2, arrive_and_go),
    )
    for part in range(GROUP):
        finish_piece(HQ - GROUP + part, part, (0,))
        send_piece(HQ - GROUP + part, lambda copy: copy.start())
    block_kept(0, True)
    stream(HK, lambda step: block_kept(step, False), lambda: None, lambda: None)
    for part in range(GROUP):
        finish_piece(HQ - GROUP + part, part, (1,))
        send_piece(HQ + part, lambda copy: copy.start())

    mean = jnp.sum(square[...], axis=-1, keepdims=True) * (1.0 / (HQ * HD))
    norm = jnp.broadcast_to(lax.rsqrt(mean + 1e-06), (rows, HALF))
    norms[secs - 1] = norm.T[:1, :]
    to_later(lambda target: norm_copy(sec, target).start())
    square[...] = norm

    pass_pieces(HK - 1, arrive_and_go)
    pass_pieces(HK, arrive_and_go)

    def wait_piece(source, piece):
        passed = (
            ((sec == 1) & (source == 0) & (piece % GROUP == 0))
            | ((sec == 2) & (source == 0) & (piece % GROUP == 1))
            | ((sec == 3) & (source == 1))
        )

        @pl.when(jnp.logical_not(passed))
        def _():
            passed_copy(source, piece, 3).wait_recv()

    def wait_pieces(pieces):
        for source in range(secs - 1):

            @pl.when(source < sec)
            def _(source=source):
                for piece in pieces:
                    wait_piece(source, piece)

    def add_layers(places):
        for layer in range(secs):

            @pl.when(sec == layer)
            def _(layer=layer):
                spread = [
                    jnp.broadcast_to(norms[k], (HALF, rows)).T for k in range(layer)
                ]
                for head, half in places:
                    cols = slice(head * HD + half * HALF, head * HD + (half + 1) * HALF)
                    total = own[head, half] * square[...] * gains[secs - 1, :, cols]
                    for k in range(layer):
                        part = got[k, head, half].astype(jnp.float32)
                        total = total + part * spread[k] * gains[k, :, cols]
                    out_ref[0, :, cols] = total.astype(jnp.bfloat16)

    for source in range(secs - 1):

        @pl.when(source < sec)
        def _(source=source):
            gain_copy(source, secs - 1).wait_recv()
            norm_copy(source, secs - 1).wait_recv()

    early, late = range(HQ - GROUP), range(HQ - GROUP, HQ)
    wait_pieces(early)
    add_layers([(head, half) for head in early for half in (0, 1)])
    for half in (0, 1):
        wait_pieces(range(HQ - GROUP + half * GROUP, HQ + half * GROUP))
        add_layers([(head, half) for head in late])

    def finish(chunk):
        def finish_step(step, carry):
            @pl.when(me >= step)
            def _():
                send_block(step, chunk, lambda copy: copy.wait_send())

            return carry

        lax.fori_loop(0, back, finish_step, 0)
        for part in range(GROUP):
            send_piece(GROUP * chunk + part, lambda copy: copy.wait_send())
        pass_pieces(chunk, lambda copy: copy.wait_send())

    def finish_head(head, carry):
        finish(head)
        return carry

    lax.fori_loop(0, HK - 1, finish_head, 0)
    finish(HK - 1)
    finish(HK)
    to_later(lambda target: gain_copy(sec, target).wait_send())
    to_later(lambda target: norm_copy(sec, target).wait_send())


def per_device(queries, keys, values, segment_ids, positions, residual_in, post_gain):
    rows = positions.shape[0]
    seqs = lax.axis_size("seq")
    secs = lax.axis_size("section")
    longest = seqs * rows // 2
    back = min((min(WINDOW, longest) - 1 + rows - 1) // rows, seqs - 1)
    hbm = pl.BlockSpec(memory_space=pltpu.HBM)
    vmem = pl.BlockSpec(memory_space=pltpu.VMEM)
    summed = pl.pallas_call(
        functools.partial(kernel, seqs, secs, back, rows),
        out_shape=pltpu.VMEM((1, rows, HQ * HD), jnp.bfloat16),
        in_specs=[hbm] * 5,
        out_specs=vmem,
        scratch_shapes=[
            pltpu.VMEM((1, rows, HQ * HD), jnp.bfloat16),
            pltpu.VMEM((HK, rows, HD), jnp.bfloat16),
            pltpu.VMEM((1, rows), jnp.int32),
            pltpu.VMEM((back + 1, HK, rows, 2 * HD), jnp.bfloat16),
            pltpu.VMEM((HK, GROUP * rows, HD), jnp.bfloat16),
            pltpu.VMEM((rows, HALF), jnp.float32),
            pltpu.VMEM((rows, HALF), jnp.float32),
            pltpu.VMEM((rows, rows), jnp.int32),
            pltpu.VMEM((GROUP * rows, HD), jnp.float32),
            pltpu.VMEM((GROUP * rows, HALF), jnp.float32),
            pltpu.VMEM((back + 1, GROUP, rows, rows), jnp.bfloat16),
            pltpu.VMEM((HQ, 2, rows, HALF), jnp.float32),
            pltpu.VMEM((HQ, 2, rows, HALF), jnp.bfloat16),
            pltpu.VMEM((secs - 1, HQ, 2, rows, HALF), jnp.bfloat16),
            pltpu.VMEM((rows, HALF), jnp.float32),
            pltpu.VMEM((secs, 1, rows), jnp.float32),
            pltpu.VMEM((secs, 1, HQ * HD), jnp.float32),
            pltpu.SemaphoreType.DMA((HK + 3,)),
            pltpu.SemaphoreType.DMA((HK,)),
            pltpu.SemaphoreType.DMA((2, back, HK + 1)),
            pltpu.SemaphoreType.DMA((back, HK + 1)),
            pltpu.SemaphoreType.DMA((2, HQ + GROUP)),
            pltpu.SemaphoreType.DMA((secs - 1, HQ + GROUP)),
            pltpu.SemaphoreType.DMA((secs - 1,)),
            pltpu.SemaphoreType.DMA((secs - 1,)),
            pltpu.SemaphoreType.DMA((secs - 1,)),
            pltpu.SemaphoreType.DMA((secs - 1,)),
        ],
        compiler_params=pltpu.CompilerParams(
            collective_id=0, has_side_effects=True, vmem_limit_bytes=60 * 2**20
        ),
    )(queries, keys, values, positions.reshape(1, rows), post_gain)
    running = summed.astype(jnp.float32) + residual_in.astype(jnp.float32)[None]
    return running.astype(jnp.bfloat16)


def solution(mesh):
    placed = (
        P("section", "seq", None),
        P("section", "seq", None),
        P("section", "seq", None),
        P("seq"),
        P("seq"),
        P("seq", None),
        P("section", None),
    )
    return jax.shard_map(
        per_device, mesh=mesh, in_specs=placed, out_specs=P("section", "seq", None), check_vma=False
    )
```

```python
import functools
import math

import jax
import jax.numpy as jnp
from jax import lax
from jax.experimental import pallas as pl
from jax.experimental.pallas import tpu as pltpu
from jax.sharding import PartitionSpec as P

HQ = 8
HK = 4
HD = 256
WINDOW = 4096
GROUP = HQ // HK
HALF = HD // 2
PAIR = GROUP * HD
MESH = pl.DeviceIdType.MESH
NT = (((1,), (1,)), ((), ()))
NN = (((1,), (0,)), ((), ()))


def cos_sin(angle):
    turns = jnp.floor(angle * (2.0 / math.pi) + 0.5)
    rest = angle - turns * 1.5703125
    rest = rest - turns * 4.837512969970703125e-4
    rest = rest - turns * 7.549789948768648e-8
    z = rest * rest
    sine = rest + rest * z * (
        -1.6666654611e-1 + z * (8.3321608736e-3 + z * -1.9515295891e-4)
    )
    cosine = (1.0 - 0.5 * z) + z * z * (
        4.166664568298827e-2 + z * (-1.388731625493765e-3 + z * 2.443315711809948e-5)
    )
    quarter = turns.astype(jnp.int32) & 3
    odd = (quarter & 1) == 1
    first = jnp.where(odd, sine, cosine)
    second = jnp.where(odd, cosine, sine)
    return (
        jnp.where((quarter == 1) | (quarter == 2), -first, first),
        jnp.where(quarter >= 2, -second, second),
    )


def kernel(
    seqs, secs, back, rows,
    q_ref, k_ref, v_ref, pos_ref, gain_ref,
    out_ref,
    q_in, k_in, pos_in, kv, qrot, cos_ref, sin_ref, low, acc, den, late_w, own, sent, got, square,
    norms, gains,
    in_sem, v_sem, kv_send, kv_recv, att_send, att_recv, gain_send, gain_recv, norm_send, norm_recv,
):
    me = lax.axis_index("seq")
    sec = lax.axis_index("section")

    barrier = pltpu.get_barrier_semaphore()

    @pl.when(me > 0)
    def _():
        pl.semaphore_signal(barrier, inc=1, device_id={"seq": me - 1}, device_id_type=MESH)

    for other in range(secs - 1):

        @pl.when(other < sec)
        def _(other=other):
            pl.semaphore_signal(barrier, inc=1, device_id={"section": other}, device_id_type=MESH)

    @pl.when(sec == 2)
    def _():
        pl.semaphore_signal(barrier, inc=1, device_id={"section": 3}, device_id_type=MESH)

    def columns(head):
        return pl.ds(head * HD, HD)

    pos_load = pltpu.make_async_copy(pos_ref, pos_in, in_sem.at[HK])
    q_load = pltpu.make_async_copy(q_ref, q_in, in_sem.at[HK + 1])
    gain_load = pltpu.make_async_copy(gain_ref, gains.at[secs - 1], in_sem.at[HK + 2])
    k_loads = [
        pltpu.make_async_copy(k_ref.at[0, :, columns(h)], k_in.at[h], in_sem.at[h])
        for h in range(HK)
    ]
    v_loads = [
        pltpu.make_async_copy(v_ref.at[0, :, columns(h)], kv.at[0, h, :, pl.ds(HD, HD)], v_sem.at[h])
        for h in range(HK)
    ]
    for load in [pos_load, k_loads[0], v_loads[0], gain_load, q_load] + k_loads[1:] + v_loads[1:]:
        load.start()

    def kv_copy(step, chunk):
        if not isinstance(chunk, int) or chunk < HK - 1:
            at = lambda block: kv.at[block, chunk]
        elif chunk == HK - 1:
            at = lambda block: kv.at[block, HK - 1, :, pl.ds(0, HD + HALF)]
        else:
            at = lambda block: kv.at[block, HK - 1, :, pl.ds(HD + HALF, HALF)]
        return pltpu.make_async_remote_copy(
            src_ref=at(step),
            dst_ref=at(step + 1),
            send_sem=kv_send.at[step, chunk],
            recv_sem=kv_recv.at[step, chunk],
            device_id={"seq": me + 1},
            device_id_type=MESH,
        )

    def piece_of(ref, piece):
        if not isinstance(piece, int) or piece < HQ - GROUP:
            return ref.at[piece]
        late = piece - (HQ - GROUP)
        return ref.at[HQ - GROUP + late % GROUP, late // GROUP]

    def own_copy(slot, source, piece, target):
        return pltpu.make_async_remote_copy(
            src_ref=piece_of(sent, piece),
            dst_ref=piece_of(got.at[source], piece),
            send_sem=att_send.at[slot, piece],
            recv_sem=att_recv.at[source, piece],
            device_id={"section": target},
            device_id_type=MESH,
        )

    def passed_copy(source, piece, target):
        return pltpu.make_async_remote_copy(
            src_ref=piece_of(got.at[source], piece),
            dst_ref=piece_of(got.at[source], piece),
            send_sem=att_send.at[1, piece],
            recv_sem=att_recv.at[source, piece],
            device_id={"section": target},
            device_id_type=MESH,
        )

    def gain_copy(source, target):
        return pltpu.make_async_remote_copy(
            src_ref=gains.at[secs - 1],
            dst_ref=gains.at[source],
            send_sem=gain_send.at[target - 1],
            recv_sem=gain_recv.at[source],
            device_id={"section": target},
            device_id_type=MESH,
        )

    def norm_copy(source, target):
        return pltpu.make_async_remote_copy(
            src_ref=norms.at[secs - 1],
            dst_ref=norms.at[source],
            send_sem=norm_send.at[target - 1],
            recv_sem=norm_recv.at[source],
            device_id={"section": target},
            device_id_type=MESH,
        )

    def to_later(act):
        for target in range(1, secs):

            @pl.when(target > sec)
            def _(target=target):
                act(target)

    def send_piece(piece, act):
        @pl.when(sec == 0)
        def _():
            act(own_copy(0, 0, piece, 1))
            act(own_copy(1, 0, piece, 2))

        @pl.when(sec == 1)
        def _():
            act(own_copy(0, 1, piece, 3))

        @pl.when(sec == 2)
        def _():
            act(own_copy(0, 2, piece, 3))

    def pass_pieces(head, act):
        @pl.when(sec == 1)
        def _():
            act(passed_copy(0, GROUP * head, 3))

        @pl.when(sec == 2)
        def _():
            act(passed_copy(0, GROUP * head + 1, 3))

        @pl.when(sec == 3)
        def _():
            for part in range(GROUP):
                act(passed_copy(1, GROUP * head + part, 2))

    def arrive_and_go(copy):
        copy.wait_recv()
        copy.start()

    pos_load.wait()
    place = jnp.broadcast_to(pos_in[...], (HALF, rows)).astype(jnp.float32).T
    lane = lax.broadcasted_iota(jnp.int32, (rows, HALF), 1).astype(jnp.float32)
    angle = place * jnp.exp(lane * (-math.log(10000.0) / HALF))
    cos_ref[...], sin_ref[...] = cos_sin(angle)

    def turned(first, second):
        first, second = first.astype(jnp.float32), second.astype(jnp.float32)
        cosine, sine = cos_ref[...], sin_ref[...]
        return (
            (first * cosine - second * sine).astype(jnp.bfloat16),
            (second * cosine + first * sine).astype(jnp.bfloat16),
        )

    def pack(head):
        k_loads[head].wait()
        first, second = turned(k_in[head, :, :HALF], k_in[head, :, HALF:])
        kv[0, head, :, :HALF] = first
        kv[0, head, :, HALF:HD] = second
        v_loads[head].wait()

    pack(0)
    expected = (
        jnp.where(me < seqs - 1, 1, 0) + (secs - 1 - sec) + jnp.where(sec == 3, 1, 0)
    )

    @pl.when(expected > 0)
    def _():
        pl.semaphore_wait(barrier, expected)

    @pl.when(me < seqs - 1)
    def _():
        kv_copy(0, 0).start()

    gain_load.wait()
    to_later(lambda target: gain_copy(sec, target).start())

    q_load.wait()
    for head in range(HQ):
        at = head * HD
        first, second = turned(q_in[0, :, at : at + HALF], q_in[0, :, at + HALF : at + HD])
        part = pl.ds((head % GROUP) * rows, rows)
        qrot[head // GROUP, part, :HALF] = first
        qrot[head // GROUP, part, HALF:] = second
    for head in range(1, HK):
        pack(head)

    reach = jnp.minimum(place, float(WINDOW - 1)).astype(jnp.int32)
    gap = lax.broadcasted_iota(jnp.int32, (rows, rows), 0) - lax.broadcasted_iota(
        jnp.int32, (rows, rows), 1
    )
    for start in range(0, rows, HALF):
        part = gap[:, start : start + HALF] - reach
        for at in range(0, GROUP * rows, rows):
            low[at : at + rows, start : start + HALF] = part
    gap = jnp.concatenate([gap] * GROUP, axis=0)

    def weights(step, head, first):
        score = lax.dot_general(
            qrot[head], kv[step, head, :, :HD], NT, preferred_element_type=jnp.float32
        )
        capped = jnp.tanh(score * (HD ** (-0.5) / 50.0))
        weight = jnp.exp2(capped * (50.0 * math.log2(math.e)))
        allowed = low[...] <= -step * rows
        if first:
            allowed = allowed & (gap >= 0)
        weight = jnp.where(allowed, weight, 0.0)
        total = weight[:, :HALF]
        for start in range(HALF, rows, HALF):
            total = total + weight[:, start : start + HALF]
        if first:
            den[...] = total
        else:
            den[...] += total
        return weight.astype(jnp.bfloat16)

    def add_values(weight, step, head, cols, first):
        summed = lax.dot_general(
            weight,
            kv[step, head, :, HD + cols.start : HD + cols.stop],
            NN,
            preferred_element_type=jnp.float32,
        )
        if first:
            acc[:, cols] = summed
        else:
            acc[:, cols] += summed

    def block(step, head, first):
        add_values(weights(step, head, first), step, head, slice(0, HD), first)

    def block_keep(step, first):
        weight = weights(step, HK - 1, first)
        late_w[step] = weight
        add_values(weight, step, HK - 1, slice(0, HALF), first)

    def block_kept(step, first):
        add_values(late_w[step], step, HK - 1, slice(HALF, HD), first)

    def start_own(chunk):
        @pl.when(me < seqs - 1)
        def _():
            kv_copy(0, chunk).start()

    def stream(chunk, work, last, passing):
        def earlier(step, carry):
            @pl.when(step == back)
            def _():
                last()

            @pl.when(me >= step)
            def _():
                kv_copy(step - 1, chunk).wait_recv()

                @pl.when((step < back) & (me < seqs - 1))
                def _():
                    kv_copy(step, chunk).start()

                work(step)

            @pl.when(step == max(back - 1, 1))
            def _():
                passing()

            return carry

        lax.fori_loop(1, back + 1, earlier, 0)

    def finish_piece(piece, part, halves):
        at = pl.ds(part * rows, rows)
        share = 1.0 / jnp.sum(den[at, :], axis=-1, keepdims=True)
        total = 0.0
        for half in halves:
            value = acc[at, half * HALF : (half + 1) * HALF] * share
            own[piece, half] = value
            sent[piece, half] = value.astype(jnp.bfloat16)
            total = total + value * value
        square[...] += total

    square[...] = jnp.zeros_like(square)

    def one_head(head, carry):
        def last():
            @pl.when(head < HK - 2)
            def _():
                start_own(head + 1)

            @pl.when(head == HK - 2)
            def _():
                start_own(HK - 1)

        def passing():
            @pl.when(head > 0)
            def _():
                pass_pieces(head - 1, arrive_and_go)

        block(0, head, True)
        stream(head, lambda step: block(step, head, False), last, passing)
        for part in range(GROUP):
            finish_piece(GROUP * head + part, part, (0, 1))
            send_piece(GROUP * head + part, lambda copy: copy.start())
        return carry

    lax.fori_loop(0, HK - 1, one_head, 0)

    block_keep(0, True)
    stream(
        HK - 1,
        lambda step: block_keep(step, False),
        lambda: start_own(HK),
        lambda: pass_pieces(HK - 2, arrive_and_go),
    )
    for part in range(GROUP):
        finish_piece(HQ - GROUP + part, part, (0,))
        send_piece(HQ - GROUP + part, lambda copy: copy.start())
    block_kept(0, True)
    stream(HK, lambda step: block_kept(step, False), lambda: None, lambda: None)
    for part in range(GROUP):
        finish_piece(HQ - GROUP + part, part, (1,))
        send_piece(HQ + part, lambda copy: copy.start())

    mean = jnp.sum(square[...], axis=-1, keepdims=True) * (1.0 / (HQ * HD))
    norm = jnp.broadcast_to(lax.rsqrt(mean + 1e-06), (rows, HALF))
    norms[secs - 1] = norm.T[:1, :]
    to_later(lambda target: norm_copy(sec, target).start())
    square[...] = norm

    pass_pieces(HK - 1, arrive_and_go)
    pass_pieces(HK, arrive_and_go)

    def wait_piece(source, piece):
        passed = (
            ((sec == 1) & (source == 0) & (piece % GROUP == 0))
            | ((sec == 2) & (source == 0) & (piece % GROUP == 1))
            | ((sec == 3) & (source == 1))
        )

        @pl.when(jnp.logical_not(passed))
        def _():
            passed_copy(source, piece, 3).wait_recv()

    def wait_pieces(pieces):
        for source in range(secs - 1):

            @pl.when(source < sec)
            def _(source=source):
                for piece in pieces:
                    wait_piece(source, piece)

    def add_layers(places):
        for layer in range(secs):

            @pl.when(sec == layer)
            def _(layer=layer):
                spread = [
                    jnp.broadcast_to(norms[k], (HALF, rows)).T for k in range(layer)
                ]
                for head, half in places:
                    cols = slice(head * HD + half * HALF, head * HD + (half + 1) * HALF)
                    total = own[head, half] * square[...] * gains[secs - 1, :, cols]
                    for k in range(layer):
                        part = got[k, head, half].astype(jnp.float32)
                        total = total + part * spread[k] * gains[k, :, cols]
                    out_ref[0, :, cols] = total.astype(jnp.bfloat16)

    for source in range(secs - 1):

        @pl.when(source < sec)
        def _(source=source):
            gain_copy(source, secs - 1).wait_recv()
            norm_copy(source, secs - 1).wait_recv()

    early, late = range(HQ - GROUP), range(HQ - GROUP, HQ)
    wait_pieces(early)
    add_layers([(head, half) for head in early for half in (0, 1)])
    for half in (0, 1):
        wait_pieces(range(HQ - GROUP + half * GROUP, HQ + half * GROUP))
        add_layers([(head, half) for head in late])

    def finish(chunk):
        def finish_step(step, carry):
            @pl.when((me >= step) & (me < seqs - 1))
            def _():
                kv_copy(step, chunk).wait_send()

            return carry

        lax.fori_loop(0, back, finish_step, 0)
        for part in range(GROUP):
            send_piece(GROUP * chunk + part, lambda copy: copy.wait_send())
        pass_pieces(chunk, lambda copy: copy.wait_send())

    def finish_head(head, carry):
        finish(head)
        return carry

    lax.fori_loop(0, HK - 1, finish_head, 0)
    finish(HK - 1)
    finish(HK)
    to_later(lambda target: gain_copy(sec, target).wait_send())
    to_later(lambda target: norm_copy(sec, target).wait_send())


def per_device(queries, keys, values, segment_ids, positions, residual_in, post_gain):
    rows = positions.shape[0]
    seqs = lax.axis_size("seq")
    secs = lax.axis_size("section")
    longest = seqs * rows // 2
    back = min((min(WINDOW, longest) - 1 + rows - 1) // rows, seqs - 1)
    hbm = pl.BlockSpec(memory_space=pltpu.HBM)
    vmem = pl.BlockSpec(memory_space=pltpu.VMEM)
    summed = pl.pallas_call(
        functools.partial(kernel, seqs, secs, back, rows),
        out_shape=pltpu.VMEM((1, rows, HQ * HD), jnp.bfloat16),
        in_specs=[hbm] * 5,
        out_specs=vmem,
        scratch_shapes=[
            pltpu.VMEM((1, rows, HQ * HD), jnp.bfloat16),
            pltpu.VMEM((HK, rows, HD), jnp.bfloat16),
            pltpu.VMEM((1, rows), jnp.int32),
            pltpu.VMEM((back + 1, HK, rows, 2 * HD), jnp.bfloat16),
            pltpu.VMEM((HK, GROUP * rows, HD), jnp.bfloat16),
            pltpu.VMEM((rows, HALF), jnp.float32),
            pltpu.VMEM((rows, HALF), jnp.float32),
            pltpu.VMEM((GROUP * rows, rows), jnp.int32),
            pltpu.VMEM((GROUP * rows, HD), jnp.float32),
            pltpu.VMEM((GROUP * rows, HALF), jnp.float32),
            pltpu.VMEM((back + 1, GROUP * rows, rows), jnp.bfloat16),
            pltpu.VMEM((HQ, 2, rows, HALF), jnp.float32),
            pltpu.VMEM((HQ, 2, rows, HALF), jnp.bfloat16),
            pltpu.VMEM((secs - 1, HQ, 2, rows, HALF), jnp.bfloat16),
            pltpu.VMEM((rows, HALF), jnp.float32),
            pltpu.VMEM((secs, 1, rows), jnp.float32),
            pltpu.VMEM((secs, 1, HQ * HD), jnp.float32),
            pltpu.SemaphoreType.DMA((HK + 3,)),
            pltpu.SemaphoreType.DMA((HK,)),
            pltpu.SemaphoreType.DMA((back, HK + 1)),
            pltpu.SemaphoreType.DMA((back, HK + 1)),
            pltpu.SemaphoreType.DMA((2, HQ + GROUP)),
            pltpu.SemaphoreType.DMA((secs - 1, HQ + GROUP)),
            pltpu.SemaphoreType.DMA((secs - 1,)),
            pltpu.SemaphoreType.DMA((secs - 1,)),
            pltpu.SemaphoreType.DMA((secs - 1,)),
            pltpu.SemaphoreType.DMA((secs - 1,)),
        ],
        compiler_params=pltpu.CompilerParams(
            collective_id=0, has_side_effects=True, vmem_limit_bytes=60 * 2**20
        ),
    )(queries, keys, values, positions.reshape(1, rows), post_gain)
    running = summed.astype(jnp.float32) + residual_in.astype(jnp.float32)[None]
    return running.astype(jnp.bfloat16)


def solution(mesh):
    placed = (
        P("section", "seq", None),
        P("section", "seq", None),
        P("section", "seq", None),
        P("seq"),
        P("seq"),
        P("seq", None),
        P("section", None),
    )
    return jax.shard_map(
        per_device, mesh=mesh, in_specs=placed, out_specs=P("section", "seq", None), check_vma=False
    )
```

```python
import functools
import math

import jax
import jax.numpy as jnp
from jax import lax
from jax.experimental import pallas as pl
from jax.experimental.pallas import tpu as pltpu
from jax.sharding import PartitionSpec as P

HQ = 8
HK = 4
HD = 256
WINDOW = 4096
GROUP = HQ // HK
HALF = HD // 2
PAIR = GROUP * HD
MESH = pl.DeviceIdType.MESH
NT = (((1,), (1,)), ((), ()))
NN = (((1,), (0,)), ((), ()))


def cos_sin(angle):
    turns = jnp.floor(angle * (2.0 / math.pi) + 0.5)
    rest = angle - turns * 1.5703125
    rest = rest - turns * 4.837512969970703125e-4
    rest = rest - turns * 7.549789948768648e-8
    z = rest * rest
    sine = rest + rest * z * (
        -1.6666654611e-1 + z * (8.3321608736e-3 + z * -1.9515295891e-4)
    )
    cosine = (1.0 - 0.5 * z) + z * z * (
        4.166664568298827e-2 + z * (-1.388731625493765e-3 + z * 2.443315711809948e-5)
    )
    quarter = turns.astype(jnp.int32) & 3
    odd = (quarter & 1) == 1
    first = jnp.where(odd, sine, cosine)
    second = jnp.where(odd, cosine, sine)
    return (
        jnp.where((quarter == 1) | (quarter == 2), -first, first),
        jnp.where(quarter >= 2, -second, second),
    )


def kernel(
    seqs, secs, back, rows,
    q_ref, k_ref, v_ref, pos_ref, gain_ref,
    out_ref,
    q_in, k_in, pos_in, kv, qrot, cos_ref, sin_ref, low, acc, den, late_w, own, sent, got, square,
    norms, gains,
    in_sem, v_sem, kv_send, kv_recv, att_send, att_recv, gain_send, gain_recv, norm_send, norm_recv,
):
    me = lax.axis_index("seq")
    sec = lax.axis_index("section")

    barrier = pltpu.get_barrier_semaphore()

    @pl.when(me > 0)
    def _():
        pl.semaphore_signal(barrier, inc=1, device_id={"seq": me - 1}, device_id_type=MESH)

    for other in range(secs - 1):

        @pl.when(other < sec)
        def _(other=other):
            pl.semaphore_signal(barrier, inc=1, device_id={"section": other}, device_id_type=MESH)

    @pl.when(sec == 2)
    def _():
        pl.semaphore_signal(barrier, inc=1, device_id={"section": 3}, device_id_type=MESH)

    def columns(head):
        return pl.ds(head * HD, HD)

    pos_load = pltpu.make_async_copy(pos_ref, pos_in, in_sem.at[HK])
    q_load = pltpu.make_async_copy(q_ref, q_in, in_sem.at[HK + 1])
    gain_load = pltpu.make_async_copy(gain_ref, gains.at[secs - 1], in_sem.at[HK + 2])
    k_loads = [
        pltpu.make_async_copy(k_ref.at[0, :, columns(h)], k_in.at[h], in_sem.at[h])
        for h in range(HK)
    ]
    v_loads = [
        pltpu.make_async_copy(v_ref.at[0, :, columns(h)], kv.at[0, h, :, pl.ds(HD, HD)], v_sem.at[h])
        for h in range(HK)
    ]
    for load in [pos_load, k_loads[0], v_loads[0], gain_load, q_load] + k_loads[1:] + v_loads[1:]:
        load.start()

    def kv_copy(step, chunk):
        if not isinstance(chunk, int) or chunk < HK - 1:
            at = lambda block: kv.at[block, chunk]
        elif chunk == HK - 1:
            at = lambda block: kv.at[block, HK - 1, :, pl.ds(0, HD + HALF)]
        else:
            at = lambda block: kv.at[block, HK - 1, :, pl.ds(HD + HALF, HALF)]
        return pltpu.make_async_remote_copy(
            src_ref=at(step),
            dst_ref=at(step + 1),
            send_sem=kv_send.at[step, chunk],
            recv_sem=kv_recv.at[step, chunk],
            device_id={"seq": me + 1},
            device_id_type=MESH,
        )

    def piece_of(ref, piece):
        if not isinstance(piece, int) or piece < HQ - GROUP:
            return ref.at[piece]
        late = piece - (HQ - GROUP)
        return ref.at[HQ - GROUP + late % GROUP, late // GROUP]

    def own_copy(slot, source, piece, target):
        return pltpu.make_async_remote_copy(
            src_ref=piece_of(sent, piece),
            dst_ref=piece_of(got.at[source], piece),
            send_sem=att_send.at[slot, piece],
            recv_sem=att_recv.at[source, piece],
            device_id={"section": target},
            device_id_type=MESH,
        )

    def passed_copy(source, piece, target):
        return pltpu.make_async_remote_copy(
            src_ref=piece_of(got.at[source], piece),
            dst_ref=piece_of(got.at[source], piece),
            send_sem=att_send.at[1, piece],
            recv_sem=att_recv.at[source, piece],
            device_id={"section": target},
            device_id_type=MESH,
        )

    def gain_copy(source, target):
        return pltpu.make_async_remote_copy(
            src_ref=gains.at[secs - 1],
            dst_ref=gains.at[source],
            send_sem=gain_send.at[target - 1],
            recv_sem=gain_recv.at[source],
            device_id={"section": target},
            device_id_type=MESH,
        )

    def norm_copy(source, target):
        return pltpu.make_async_remote_copy(
            src_ref=norms.at[secs - 1],
            dst_ref=norms.at[source],
            send_sem=norm_send.at[target - 1],
            recv_sem=norm_recv.at[source],
            device_id={"section": target},
            device_id_type=MESH,
        )

    def to_later(act):
        for target in range(1, secs):

            @pl.when(target > sec)
            def _(target=target):
                act(target)

    def send_piece(piece, act):
        @pl.when(sec == 0)
        def _():
            act(own_copy(0, 0, piece, 1))
            act(own_copy(1, 0, piece, 2))

        @pl.when(sec == 1)
        def _():
            act(own_copy(0, 1, piece, 3))

        @pl.when(sec == 2)
        def _():
            act(own_copy(0, 2, piece, 3))

    def pass_pieces(head, act):
        @pl.when(sec == 1)
        def _():
            act(passed_copy(0, GROUP * head, 3))

        @pl.when(sec == 2)
        def _():
            act(passed_copy(0, GROUP * head + 1, 3))

        @pl.when(sec == 3)
        def _():
            for part in range(GROUP):
                act(passed_copy(1, GROUP * head + part, 2))

    def arrive_and_go(copy):
        copy.wait_recv()
        copy.start()

    pos_load.wait()
    place = jnp.broadcast_to(pos_in[...], (HALF, rows)).astype(jnp.float32).T
    lane = lax.broadcasted_iota(jnp.int32, (rows, HALF), 1).astype(jnp.float32)
    angle = place * jnp.exp(lane * (-math.log(10000.0) / HALF))
    cos_ref[...], sin_ref[...] = cos_sin(angle)

    def turned(first, second):
        first, second = first.astype(jnp.float32), second.astype(jnp.float32)
        cosine, sine = cos_ref[...], sin_ref[...]
        return (
            (first * cosine - second * sine).astype(jnp.bfloat16),
            (second * cosine + first * sine).astype(jnp.bfloat16),
        )

    def pack(head):
        k_loads[head].wait()
        first, second = turned(k_in[head, :, :HALF], k_in[head, :, HALF:])
        kv[0, head, :, :HALF] = first
        kv[0, head, :, HALF:HD] = second
        v_loads[head].wait()

    pack(0)
    expected = (
        jnp.where(me < seqs - 1, 1, 0) + (secs - 1 - sec) + jnp.where(sec == 3, 1, 0)
    )

    @pl.when(expected > 0)
    def _():
        pl.semaphore_wait(barrier, expected)

    @pl.when(me < seqs - 1)
    def _():
        kv_copy(0, 0).start()

    gain_load.wait()
    to_later(lambda target: gain_copy(sec, target).start())

    q_load.wait()
    for head in range(HQ):
        at = head * HD
        first, second = turned(q_in[0, :, at : at + HALF], q_in[0, :, at + HALF : at + HD])
        part = pl.ds((head % GROUP) * rows, rows)
        qrot[head // GROUP, part, :HALF] = first
        qrot[head // GROUP, part, HALF:] = second
    for head in range(1, HK):
        pack(head)

    reach = jnp.minimum(place, float(WINDOW - 1)).astype(jnp.int32)
    gap = lax.broadcasted_iota(jnp.int32, (rows, rows), 0) - lax.broadcasted_iota(
        jnp.int32, (rows, rows), 1
    )
    for start in range(0, rows, HALF):
        part = gap[:, start : start + HALF] - reach
        for at in range(0, GROUP * rows, rows):
            low[at : at + rows, start : start + HALF] = part
    gap = jnp.concatenate([gap] * GROUP, axis=0)

    def weights(step, head, first):
        score = lax.dot_general(
            qrot[head], kv[step, head, :, :HD], NT, preferred_element_type=jnp.float32
        )
        capped = jnp.tanh(score * (HD ** (-0.5) / 50.0))
        weight = jnp.exp2(capped * (50.0 * math.log2(math.e)))
        allowed = low[...] <= -step * rows
        if first:
            allowed = allowed & (gap >= 0)
        weight = jnp.where(allowed, weight, 0.0)
        total = weight[:, :HALF]
        for start in range(HALF, rows, HALF):
            total = total + weight[:, start : start + HALF]
        if first:
            den[...] = total
        else:
            den[...] += total
        return weight.astype(jnp.bfloat16)

    def add_values(weight, step, head, cols, first):
        summed = lax.dot_general(
            weight,
            kv[step, head, :, HD + cols.start : HD + cols.stop],
            NN,
            preferred_element_type=jnp.float32,
        )
        if first:
            acc[:, cols] = summed
        else:
            acc[:, cols] += summed

    def block(step, head, first):
        add_values(weights(step, head, first), step, head, slice(0, HD), first)

    def block_keep(step, first):
        weight = weights(step, HK - 1, first)
        late_w[step] = weight
        add_values(weight, step, HK - 1, slice(0, HALF), first)

    def block_kept(step, first):
        add_values(late_w[step], step, HK - 1, slice(HALF, HD), first)

    def start_own(chunk):
        @pl.when(me < seqs - 1)
        def _():
            kv_copy(0, chunk).start()

    def stream(chunk, work, last, passing):
        def earlier(step, carry):
            @pl.when(step == back)
            def _():
                last()

            @pl.when(me >= step)
            def _():
                kv_copy(step - 1, chunk).wait_recv()

                @pl.when((step < back) & (me < seqs - 1))
                def _():
                    kv_copy(step, chunk).start()

                work(step)

            @pl.when(step == max(back - 1, 1))
            def _():
                passing()

            return carry

        lax.fori_loop(1, back + 1, earlier, 0)

    def finish_piece(piece, part, halves):
        at = pl.ds(part * rows, rows)
        share = 1.0 / jnp.sum(den[at, :], axis=-1, keepdims=True)
        total = 0.0
        for half in halves:
            value = acc[at, half * HALF : (half + 1) * HALF] * share
            own[piece, half] = value
            sent[piece, half] = value.astype(jnp.bfloat16)
            total = total + value * value
        square[...] += total

    square[...] = jnp.zeros_like(square)

    def one_head(head, carry):
        def last():
            @pl.when(head < HK - 2)
            def _():
                start_own(head + 1)

            @pl.when(head == HK - 2)
            def _():
                start_own(HK - 1)

        def passing():
            @pl.when(head > 0)
            def _():
                pass_pieces(head - 1, arrive_and_go)

        block(0, head, True)
        stream(head, lambda step: block(step, head, False), last, passing)
        for part in range(GROUP):
            finish_piece(GROUP * head + part, part, (0, 1))
            send_piece(GROUP * head + part, lambda copy: copy.start())
        return carry

    lax.fori_loop(0, HK - 1, one_head, 0)

    def late_arrives(step):
        kv_copy(step - 1, HK).wait_recv()

        @pl.when((step < back) & (me < seqs - 1))
        def _():
            kv_copy(step, HK).start()

    def last_head(step, carry):
        @pl.when(me >= step)
        def _():
            kv_copy(step - 1, HK - 1).wait_recv()

            @pl.when((step < back) & (me < seqs - 1))
            def _():
                kv_copy(step, HK - 1).start()

        @pl.when(step == 1)
        def _():
            start_own(HK)

        @pl.when((step > 1) & (me >= step - 1))
        def _():
            late_arrives(step - 1)

        @pl.when(me >= step)
        def _():
            block_keep(step, False)

        @pl.when(step == max(back - 1, 1))
        def _():
            pass_pieces(HK - 2, arrive_and_go)

        return carry

    def last_values(step, carry):
        @pl.when((step == back) & (me >= step))
        def _():
            late_arrives(step)

        @pl.when(me >= step)
        def _():
            block_kept(step, False)

        return carry

    block_keep(0, True)
    lax.fori_loop(1, back + 1, last_head, 0)
    for part in range(GROUP):
        finish_piece(HQ - GROUP + part, part, (0,))
        send_piece(HQ - GROUP + part, lambda copy: copy.start())
    block_kept(0, True)
    lax.fori_loop(1, back + 1, last_values, 0)
    for part in range(GROUP):
        finish_piece(HQ - GROUP + part, part, (1,))
        send_piece(HQ + part, lambda copy: copy.start())

    mean = jnp.sum(square[...], axis=-1, keepdims=True) * (1.0 / (HQ * HD))
    norm = jnp.broadcast_to(lax.rsqrt(mean + 1e-06), (rows, HALF))
    norms[secs - 1] = norm.T[:1, :]
    to_later(lambda target: norm_copy(sec, target).start())
    square[...] = norm

    pass_pieces(HK - 1, arrive_and_go)
    pass_pieces(HK, arrive_and_go)

    def wait_piece(source, piece):
        passed = (
            ((sec == 1) & (source == 0) & (piece % GROUP == 0))
            | ((sec == 2) & (source == 0) & (piece % GROUP == 1))
            | ((sec == 3) & (source == 1))
        )

        @pl.when(jnp.logical_not(passed))
        def _():
            passed_copy(source, piece, 3).wait_recv()

    def wait_pieces(pieces):
        for source in range(secs - 1):

            @pl.when(source < sec)
            def _(source=source):
                for piece in pieces:
                    wait_piece(source, piece)

    def add_layers(places):
        for layer in range(secs):

            @pl.when(sec == layer)
            def _(layer=layer):
                spread = [
                    jnp.broadcast_to(norms[k], (HALF, rows)).T for k in range(layer)
                ]
                for head, half in places:
                    cols = slice(head * HD + half * HALF, head * HD + (half + 1) * HALF)
                    total = own[head, half] * square[...] * gains[secs - 1, :, cols]
                    for k in range(layer):
                        part = got[k, head, half].astype(jnp.float32)
                        total = total + part * spread[k] * gains[k, :, cols]
                    out_ref[0, :, cols] = total.astype(jnp.bfloat16)

    for source in range(secs - 1):

        @pl.when(source < sec)
        def _(source=source):
            gain_copy(source, secs - 1).wait_recv()
            norm_copy(source, secs - 1).wait_recv()

    early, late = range(HQ - GROUP), range(HQ - GROUP, HQ)
    wait_pieces(early)
    add_layers([(head, half) for head in early for half in (0, 1)])
    for half in (0, 1):
        wait_pieces(range(HQ - GROUP + half * GROUP, HQ + half * GROUP))
        add_layers([(head, half) for head in late])

    def finish(chunk):
        def finish_step(step, carry):
            @pl.when((me >= step) & (me < seqs - 1))
            def _():
                kv_copy(step, chunk).wait_send()

            return carry

        lax.fori_loop(0, back, finish_step, 0)
        for part in range(GROUP):
            send_piece(GROUP * chunk + part, lambda copy: copy.wait_send())
        pass_pieces(chunk, lambda copy: copy.wait_send())

    def finish_head(head, carry):
        finish(head)
        return carry

    lax.fori_loop(0, HK - 1, finish_head, 0)
    finish(HK - 1)
    finish(HK)
    to_later(lambda target: gain_copy(sec, target).wait_send())
    to_later(lambda target: norm_copy(sec, target).wait_send())


def per_device(queries, keys, values, segment_ids, positions, residual_in, post_gain):
    rows = positions.shape[0]
    seqs = lax.axis_size("seq")
    secs = lax.axis_size("section")
    longest = seqs * rows // 2
    back = min((min(WINDOW, longest) - 1 + rows - 1) // rows, seqs - 1)
    hbm = pl.BlockSpec(memory_space=pltpu.HBM)
    vmem = pl.BlockSpec(memory_space=pltpu.VMEM)
    summed = pl.pallas_call(
        functools.partial(kernel, seqs, secs, back, rows),
        out_shape=pltpu.VMEM((1, rows, HQ * HD), jnp.bfloat16),
        in_specs=[hbm] * 5,
        out_specs=vmem,
        scratch_shapes=[
            pltpu.VMEM((1, rows, HQ * HD), jnp.bfloat16),
            pltpu.VMEM((HK, rows, HD), jnp.bfloat16),
            pltpu.VMEM((1, rows), jnp.int32),
            pltpu.VMEM((back + 1, HK, rows, 2 * HD), jnp.bfloat16),
            pltpu.VMEM((HK, GROUP * rows, HD), jnp.bfloat16),
            pltpu.VMEM((rows, HALF), jnp.float32),
            pltpu.VMEM((rows, HALF), jnp.float32),
            pltpu.VMEM((GROUP * rows, rows), jnp.int32),
            pltpu.VMEM((GROUP * rows, HD), jnp.float32),
            pltpu.VMEM((GROUP * rows, HALF), jnp.float32),
            pltpu.VMEM((back + 1, GROUP * rows, rows), jnp.bfloat16),
            pltpu.VMEM((HQ, 2, rows, HALF), jnp.float32),
            pltpu.VMEM((HQ, 2, rows, HALF), jnp.bfloat16),
            pltpu.VMEM((secs - 1, HQ, 2, rows, HALF), jnp.bfloat16),
            pltpu.VMEM((rows, HALF), jnp.float32),
            pltpu.VMEM((secs, 1, rows), jnp.float32),
            pltpu.VMEM((secs, 1, HQ * HD), jnp.float32),
            pltpu.SemaphoreType.DMA((HK + 3,)),
            pltpu.SemaphoreType.DMA((HK,)),
            pltpu.SemaphoreType.DMA((back, HK + 1)),
            pltpu.SemaphoreType.DMA((back, HK + 1)),
            pltpu.SemaphoreType.DMA((2, HQ + GROUP)),
            pltpu.SemaphoreType.DMA((secs - 1, HQ + GROUP)),
            pltpu.SemaphoreType.DMA((secs - 1,)),
            pltpu.SemaphoreType.DMA((secs - 1,)),
            pltpu.SemaphoreType.DMA((secs - 1,)),
            pltpu.SemaphoreType.DMA((secs - 1,)),
        ],
        compiler_params=pltpu.CompilerParams(
            collective_id=0, has_side_effects=True, vmem_limit_bytes=60 * 2**20
        ),
    )(queries, keys, values, positions.reshape(1, rows), post_gain)
    running = summed.astype(jnp.float32) + residual_in.astype(jnp.float32)[None]
    return running.astype(jnp.bfloat16)


def solution(mesh):
    placed = (
        P("section", "seq", None),
        P("section", "seq", None),
        P("section", "seq", None),
        P("seq"),
        P("seq"),
        P("seq", None),
        P("section", None),
    )
    return jax.shard_map(
        per_device, mesh=mesh, in_specs=placed, out_specs=P("section", "seq", None), check_vma=False
    )
```
